256 devices in a mesh: gx: 4 (over y), gy: 8 (over x, z_hi), gz: 8 (over z_lo, core).
Axes of the slice: x: 4, y: 4, z: 8 (z_hi: 2, z_lo: 4; z = z_hi * 4 + z_lo), core: 2. Of those that a mesh axis runs over, the one named last changes fastest.
Arguments:
- noisy: float32 [128, 128, 1024], P('gz', 'gx', 'gy'), may hold values from -6 to 6
Outputs:
- denoised: float32 [128, 128, 1024], P('gz', 'gx', 'gy')
The draws below stay inside these ranges and needn't reach their ends.
All inputs are finite; a program needn't handle non-finite values.
Results may differ from the reference program's by a relative error of at most 0.0003.
Values sent between devices are 32-bit elements; how exact they have to be, the bound alone decides.
A program may use at most 64 MiB of HBM per device.

```python
import jax
import jax.numpy as jnp

NZ = 128
NX = 128
NY = 1024


def shard_levels(stream_key, shape, pieces, low, high):
    gain = 1.0
    for dim, shards_of in pieces:
        steps = jax.random.uniform(jax.random.fold_in(jax.random.fold_in(stream_key, 6), dim), (shards_of,), jnp.float32, low / len(pieces), high / len(pieces))
        gain = gain * jnp.repeat(jnp.exp(steps), shape[dim] // shards_of).reshape((-1,) + (1,) * (len(shape) - 1 - dim))
    return gain


def scatter_about(own_key, shape, deviation, bound, pieces=(), kind=jnp.bfloat16):
    entries = deviation * jax.random.normal(own_key, shape, jnp.float32)
    if pieces:
        entries = entries * shard_levels(own_key, shape, pieces, -0.22, 0.18)
    return jnp.clip(entries, -bound, bound).astype(kind)


def setup_inputs(seed: int = 0) -> dict:
    keys = jax.random.split(jax.random.key(seed), 2)
    noisy = scatter_about(keys[0], (NZ, NX, NY), 1.0, 6.0, ((0, 8), (1, 4), (2, 8)), jnp.float32)
    return {"noisy": noisy}


HALF_OFFSETS = [(step_z, step_x, step_y) for step_z in (-1, 0, 1) for step_x in (-1, 0, 1) for step_y in (-1, 0, 1) if (step_z, step_x, step_y) > (0, 0, 0)]
INV_PATCH = 1.0 / 343.0


def box_sum(field):
    length = field.shape[0] - 6
    total = field[0:length]
    for shift_by in range(1, 7):
        total = total + field[shift_by:shift_by + length]
    length = field.shape[1] - 6
    second = total[:, 0:length]
    for shift_by in range(1, 7):
        second = second + total[:, shift_by:shift_by + length]
    length = field.shape[2] - 6
    third = second[:, :, 0:length]
    for shift_by in range(1, 7):
        third = third + second[:, :, shift_by:shift_by + length]
    return third


def pair_weights(extended, start, extent, offset):
    low = start - 3
    base = extended[low:low + extent[0] + 6, low:low + extent[1] + 6, low:low + extent[2] + 6]
    moved = extended[low + offset[0]:low + offset[0] + extent[0] + 6, low + offset[1]:low + offset[1] + extent[1] + 6, low + offset[2]:low + offset[2] + extent[2] + 6]
    diff = base - moved
    return jnp.exp(-box_sum(diff * diff) * INV_PATCH)


def inside(start, length, total):
    coords = start + jnp.arange(length, dtype=jnp.int32)
    return ((coords >= 0) & (coords < total)).astype(jnp.float32)


def reference(noisy):
    size_z, size_x, size_y = noisy.shape
    padded = jnp.pad(noisy, 4)
    region = inside(-1, size_z + 2, size_z)[:, None, None] * inside(-1, size_x + 2, size_x)[None, :, None] * inside(-1, size_y + 2, size_y)[None, None, :]
    numerator = jnp.zeros(noisy.shape, jnp.float32)
    weight_sum = jnp.zeros(noisy.shape, jnp.float32)
    for offset in HALF_OFFSETS:
        weights = pair_weights(padded, 4, noisy.shape, offset)
        weights = weights * region[1 + offset[0]:1 + offset[0] + size_z, 1 + offset[1]:1 + offset[1] + size_x, 1 + offset[2]:1 + offset[2] + size_y]
        partner = padded[4 + offset[0]:4 + offset[0] + size_z, 4 + offset[1]:4 + offset[1] + size_x, 4 + offset[2]:4 + offset[2] + size_y]
        numerator = numerator + weights * partner
        weight_sum = weight_sum + weights
        given = jnp.pad(weights * noisy, 1)
        given_w = jnp.pad(weights, 1)
        numerator = numerator + given[1 - offset[0]:1 - offset[0] + size_z, 1 - offset[1]:1 - offset[1] + size_x, 1 - offset[2]:1 - offset[2] + size_y]
        weight_sum = weight_sum + given_w[1 - offset[0]:1 - offset[0] + size_z, 1 - offset[1]:1 - offset[1] + size_x, 1 - offset[2]:1 - offset[2] + size_y]
    return (noisy + numerator) / (1.0 + weight_sum)
```

```python
import functools
import math

import jax
import jax.numpy as jnp
import ml_dtypes
import numpy as np
from jax import lax
from jax.experimental import pallas as pl
from jax.experimental.pallas import tpu as pltpu
from jax.sharding import PartitionSpec as P

GROUPS = ((0, 0), (0, 1), (1, -1), (1, 0), (1, 1))
VARIANTS = tuple((dz, dx) for dz in (-1, 0, 1) for dx in (-1, 0, 1))
SCALE = math.sqrt(math.log2(math.e) / 343.0)
SZ, SX, SY = 16, 32, 128
BASE, PITCH = 16, 64
MASKED = -1000.0
MESH = pl.DeviceIdType.MESH
F32, BF16 = jnp.float32, jnp.bfloat16


def box_tables():
    n = np.arange(256)
    k = np.arange(512)
    j = np.arange(256)
    zk, xk = k // 32, k % 32
    zj, s = j // 8, j % 8
    xj = np.where(s < 4, 32 + s, s - 8)
    planes, rims = [], []
    for dz, dx in GROUPS:
        xc = n % 32 - dx
        zc = 4 + n // 32 - dz
        near = (abs(zk[:, None] - zc) <= 3) & (abs(xk[:, None] - xc) <= 3)
        planes.append(-near.astype(np.float32))
        halves = []
        for half in range(2):
            near = (abs(zj[:, None] - zc - 8 * half) <= 3) & (abs(xj[:, None] - xc) <= 3) & (j < 192)[:, None]
            halves.append(-near.astype(np.float32))
        rims.append(np.stack(halves))
    return np.stack(planes).astype(ml_dtypes.bfloat16), np.stack(rims).astype(ml_dtypes.bfloat16)


def iota(shape, dim):
    return lax.broadcasted_iota(jnp.int32, shape, dim)


def kernel(x_ref, wp_hbm, wh_hbm, out_ref, ext, xs_lo, xs_hi, xp, xm, ys_lo, ys_hi, yr_lo, yr_hi,
           shifted, rows_h, wp, wh, lhs, dist, num, wsum, local_sem, send_sem, recv_sem):
    gx, gy, gz = lax.axis_index("gx"), lax.axis_index("gy"), lax.axis_index("gz")
    nx, ny, nz = lax.axis_size("gx"), lax.axis_size("gy"), lax.axis_size("gz")

    own = pltpu.make_async_copy(x_ref, ext.at[pl.ds(4, SZ), pl.ds(BASE, SX), :], local_sem.at[0])
    own.start()
    tables = [pltpu.make_async_copy(wp_hbm, wp, local_sem.at[1]), pltpu.make_async_copy(wh_hbm, wh, local_sem.at[2])]
    for copy in tables:
        copy.start()

    ext[0:4] = jnp.zeros((4, PITCH, 128), F32)
    ext[20:26] = jnp.zeros((6, PITCH, 128), F32)
    ext[4:20, 0:BASE] = jnp.zeros((SZ, BASE, 128), F32)
    ext[4:20, BASE + SX:PITCH] = jnp.zeros((SZ, PITCH - BASE - SX, 128), F32)
    xp[...] = jnp.zeros_like(xp)
    xm[...] = jnp.zeros_like(xm)
    yr_lo[...] = jnp.zeros_like(yr_lo)
    yr_hi[...] = jnp.zeros_like(yr_hi)

    z_ok = {-1: gz > 0, 0: True, 1: gz < nz - 1}
    x_ok = {-1: gx > 0, 0: True, 1: gx < nx - 1}
    y_ok = {-1: gy > 0, 1: gy < ny - 1}

    def both(a, b):
        if a is True:
            return b
        if b is True:
            return a
        return jnp.logical_and(a, b)

    barrier = pltpu.get_barrier_semaphore()
    around = [(dz, dx) for dz in (-1, 0, 1) for dx in (-1, 0, 1) if (dz, dx) != (0, 0)]
    for dz, dx in around:
        @pl.when(both(z_ok[dz], x_ok[dx]))
        def _():
            pl.semaphore_signal(barrier, inc=1, device_id=(gx + dx, gy, gz + dz), device_id_type=MESH)
    for dy in (-1, 1):
        @pl.when(y_ok[dy])
        def _():
            pl.semaphore_signal(barrier, inc=1, device_id=(gx, gy + dy, gz), device_id_type=MESH)

    def count(ok):
        return ok[-1].astype(jnp.int32) + ok[1].astype(jnp.int32)

    own.wait()
    xs_lo[...] = ext[4:20, BASE:BASE + 4, :]
    xs_hi[...] = ext[4:20, BASE + 28:BASE + 32, :]
    pl.semaphore_wait(barrier, (1 + count(z_ok)) * (1 + count(x_ok)) - 1 + count(y_ok))

    def parts(dz, dx):
        send_z = {-1: slice(0, 4), 0: slice(0, 16), 1: slice(12, 16)}[dz]
        land_z = {-1: slice(20, 24), 0: slice(4, 20), 1: slice(0, 4)}[dz]
        send_z = pl.ds(send_z.start, send_z.stop - send_z.start)
        land_z = pl.ds(land_z.start, land_z.stop - land_z.start)
        if dx == 0:
            return x_ref.at[send_z], ext.at[land_z, pl.ds(BASE, SX), :]
        if dx == -1:
            return xs_lo.at[send_z], xp.at[land_z]
        return xs_hi.at[send_z], xm.at[land_z]

    copies = []
    for i, (dz, dx) in enumerate(around):
        src, dst = parts(dz, dx)
        copy = pltpu.make_async_remote_copy(
            src_ref=src, dst_ref=dst, send_sem=send_sem.at[i], recv_sem=recv_sem.at[i],
            device_id=(gx + dx, gy, gz + dz), device_id_type=MESH)
        copies.append((copy, dz, dx))
        pl.when(both(z_ok[dz], x_ok[dx]))(copy.start)
    for copy, dz, dx in copies:
        pl.when(both(z_ok[-dz], x_ok[-dx]))(copy.wait_recv)
    ext[0:24, BASE + 32:BASE + 36, :] = xp[...]
    ext[0:24, BASE - 4:BASE, :] = xm[...]

    lane = iota((128, 128), 1)
    low_half = iota((8, 128), 0) < 4

    def block(v, k):
        dz, dx = VARIANTS[v]
        if k < 6:
            return jnp.concatenate([ext[4 * k + j + dz, BASE + dx:BASE + 32 + dx, :] for j in range(4)], axis=0)
        pieces = []
        for j in range(16 if k == 6 else 8):
            zi = 16 * (k - 6) + j + dz
            pieces.append(jnp.where(low_half, ext[zi, BASE + 32 + dx:BASE + 40 + dx, :], ext[zi, BASE - 8 + dx:BASE + dx, :]))
        if k == 7:
            pieces.append(jnp.zeros((64, 128), F32))
        return jnp.concatenate(pieces, axis=0)

    def place(v, k):
        turned = (block(v, k) * SCALE).T
        if k == 7 and v > 4:
            turned = jnp.where(lane == 64 + v - 4, 1.0, turned)
        for c in range(8):
            shifted[v, k, pl.ds(8 + c, 16, stride=8), :] = turned[16 * c:16 * c + 16]
        return turned

    for k in range(8):
        turned = place(4, k)
        ys_lo[k] = turned[0:4]
        ys_hi[k] = turned[124:128]
    y_copies = []
    for i, (dy, src, dst) in enumerate(((-1, ys_lo, yr_hi), (1, ys_hi, yr_lo))):
        copy = pltpu.make_async_remote_copy(
            src_ref=src, dst_ref=dst, send_sem=send_sem.at[8 + i], recv_sem=recv_sem.at[8 + i],
            device_id=(gx, gy + dy, gz), device_id_type=MESH)
        y_copies.append((copy, dy))
        pl.when(y_ok[dy])(copy.start)
    for v in range(9):
        if v != 4:
            for k in (range(8) if v > 4 else range(1, 5)):
                place(v, k)

    for copy in tables:
        copy.wait()
    row = iota((16, 256), 0)
    col = iota((16, 256), 1)
    row_dz = jnp.where(row >= 2, 1, 0)
    row_dx = jnp.where(row == 1, 1, jnp.where((row >= 2) & (row < 5), row - 3, 0))
    known = (row >= 1) & (row < 5)
    for half in range(2):
        vz = gz * SZ + 8 * half + col // 32
        vx = gx * SX + col % 32

        def outside(sign):
            z, x = vz + sign * row_dz, vx + sign * row_dx
            return (z < 0) | (z >= nz * SZ) | (x < 0) | (x >= nx * SX)

        wh[0, half, 192:208, :] = jnp.where(known & outside(1), MASKED, 0.0).astype(BF16)
        back = known & outside(-1)
        for g in range(1, 5):
            wh[g, half, 192:208, :] = jnp.where(back & (row == g), MASKED, 0.0).astype(BF16)

    for copy, dy in y_copies:
        pl.when(y_ok[-dy])(copy.wait_recv)
    for i in range(4):
        for k in range(8):
            rows_h[4, k, (2 + 2 * i) % 8:(2 + 2 * i) % 8 + 1, :] = yr_lo[k, i:i + 1, :]
            rows_h[4, k, 7 - 2 * i:8 - 2 * i, :] = yr_hi[k, i:i + 1, :]
    lane8 = iota((8, 128), 1)
    sub = iota((8, 128), 0)

    def turn(value, by, axis):
        by = by % value.shape[axis]
        return value if by == 0 else pltpu.roll(value, by, axis)

    for dx in (-1, 1):
        v = 4 + dx
        for k in range(6):
            value = turn(rows_h[4, k], -dx, 1)
            edge = 31 if dx == 1 else 0
            source = rows_h[4, 6 + k // 4]
            for j in range(4):
                src_lane = (4 * (k % 4) + j) * 8 + (0 if dx == 1 else 7)
                dst_lane = 32 * j + edge
                value = jnp.where(lane8 == dst_lane, turn(source, dst_lane - src_lane, 1), value)
            rows_h[v, k] = value
        for m in range(2):
            value = turn(rows_h[4, 6 + m], -dx, 1)
            for zz in range(16 if m == 0 else 8):
                k = 4 * m + zz // 4
                src_lane = 32 * (zz % 4) + (0 if dx == 1 else 31)
                dst_lane = 8 * zz + (7 if dx == 1 else 0)
                value = jnp.where(lane8 == dst_lane, turn(rows_h[4, k], dst_lane - src_lane, 1), value)
            rows_h[v, 6 + m] = value
    for dx in (-1, 0, 1):
        for k in range(6):
            here = turn(rows_h[4 + dx, k], -32, 1)
            after = turn(rows_h[4 + dx, k + 1], -32, 1) if k < 5 else here
            rows_h[7 + dx, k] = jnp.where(lane8 < 96, here, after)
            if 1 <= k <= 4:
                here = turn(rows_h[4 + dx, k], 32, 1)
                before = turn(rows_h[4 + dx, k - 1], 32, 1)
                rows_h[1 + dx, k] = jnp.where(lane8 >= 32, here, before)
        here, after = turn(rows_h[4 + dx, 6], -8, 1), turn(rows_h[4 + dx, 7], -8, 1)
        rows_h[7 + dx, 6] = jnp.where(lane8 < 120, here, after)
        rows_h[7 + dx, 7] = after
    for v in range(5, 9):
        rows_h[v, 7] = jnp.where(lane8 >= 64, jnp.where(lane8 == 64 + v - 4, 1.0, 0.0), rows_h[v, 7])
    rows_h[4, 7] = jnp.where(lane8 >= 64, 0.0, rows_h[4, 7])

    for v in range(9):
        for k in (range(8) if v >= 4 else range(1, 5)):
            shifted[v, k, 0:8, :] = jnp.where(sub == 0, rows_h[v, k], turn(shifted[v, k, 128:136, :], 1, 0))
            shifted[v, k, 136:144, :] = jnp.where(sub == 7, rows_h[v, k], turn(shifted[v, k, 8:16, :], -1, 0))

    odd = sub % 2 == 1

    def halo_rows(v, k, dy):
        value = rows_h[v, k]
        if dy == 0:
            return value
        up, down = turn(value, 2, 0), turn(value, -2, 0)
        if dy == 1:
            return jnp.where(odd, up, jnp.where(sub == 0, shifted[v, k, 8:16, :], down))
        return jnp.where(odd, jnp.where(sub == 7, shifted[v, k, 128:136, :], down), up)

    def build(g, dys):
        v = g + 4
        for d, dy in enumerate(dys):
            for k in range(8):
                lanes = slice(128 * k, 128 * k + 128)
                error = None
                for j in range(8):
                    diff = shifted[4, k, 8 + 16 * j:24 + 16 * j, :] - shifted[v, k, 8 + 16 * j + 8 * dy:24 + 16 * j + 8 * dy, :]
                    square = diff * diff
                    if error is not None:
                        square = square + error
                    rounded = square.astype(BF16)
                    lhs[128 * d + 16 * j:128 * d + 16 * j + 16, lanes] = rounded
                    error = square - rounded.astype(F32)
                diff = rows_h[4, k] - halo_rows(v, k, dy)
                square = diff * diff
                high = square.astype(BF16).astype(F32)
                at = 128 * len(dys) + 16 * d
                lhs[at:at + 16, lanes] = jnp.concatenate([high, square - high], axis=0).astype(BF16)

    def multiply(g, rows):
        for w, table in enumerate((0, g)):
            if w == 1 and g == 0:
                continue
            for half in range(2):
                total = jnp.dot(lhs[0:rows, 256 * half:256 * half + 512], wp[table], preferred_element_type=F32)
                total = total + jnp.dot(lhs[0:rows, 768:1024], wh[table, half], preferred_element_type=F32)
                dist[w, 0:rows, 256 * half:256 * half + 256] = total

    keep_lo = jnp.where((sub == 0) & (gy == 0), 0.0, 1.0)
    keep_hi = jnp.where((sub == 7) & (gy == ny - 1), 0.0, 1.0)

    def weights(w, d, at, n, first):
        lanes = slice(128 * n, 128 * n + 128)
        halo = dist[w, at:at + 8, lanes] + dist[w, at + 8:at + 16, lanes]
        cache = {}

        def get(t):
            if t in cache:
                return cache[t]
            if 0 <= t < 16:
                value = dist[w, 128 * d + 8 * t:128 * d + 8 * t + 8, lanes]
            elif t < 0:
                value = jnp.where(sub == 0, turn(halo, 2 * (-t - 1), 0), turn(get(16 + t), 1, 0))
            else:
                value = jnp.where(sub == 7, turn(halo, 2 * (t - 16), 0), turn(get(t - 16), -1, 0))
            cache[t] = value
            return value

        total = get(first - 3)
        for t in range(first - 2, first + 4):
            total = total + get(t)
        result = [jnp.exp2(total)]
        for t in range(first + 1, first + 16):
            total = total + (get(t + 3) - get(t - 4))
            result.append(jnp.exp2(total))
        return result

    def gather(g, dys, start):
        v = g + 4
        for n in range(4):
            lanes = slice(128 * n, 128 * n + 128)
            for d, dy in enumerate(dys):
                at = 128 * len(dys) + 16 * d
                ahead = weights(0, d, at, n, 0)
                behind = weights(1 if g else 0, d, at, n, -dy)
                if dy == 1:
                    ahead[15] = ahead[15] * keep_hi
                    behind[0] = behind[0] * keep_lo
                elif dy == -1:
                    ahead[0] = ahead[0] * keep_lo
                    behind[15] = behind[15] * keep_hi
                for t in range(16):
                    rows = slice(8 * t, 8 * t + 8)
                    up = shifted[v, n + 1, 8 + 8 * (t + dy):16 + 8 * (t + dy), :]
                    down = shifted[8 - v, n + 1, 8 + 8 * (t - dy):16 + 8 * (t - dy), :]
                    part = ahead[t] * up + behind[t] * down
                    part_w = ahead[t] + behind[t]
                    if start and d == 0:
                        num[rows, lanes] = part
                        wsum[rows, lanes] = part_w
                    else:
                        num[rows, lanes] += part
                        wsum[rows, lanes] += part_w

    for g in range(5):
        dys = (1,) if g == 0 else (-1, 0, 1)
        build(g, dys)
        multiply(g, 144 * len(dys))
        gather(g, dys, g == 0)

    for n in range(4):
        lanes = slice(128 * n, 128 * n + 128)
        top = shifted[4, n + 1, 8:136, :] + num[:, lanes]
        shifted[0, n + 1, 8:136, :] = top * (1.0 / SCALE) / (1.0 + wsum[:, lanes])
        ordered = jnp.concatenate([shifted[0, n + 1, pl.ds(8 + c, 16, stride=8), :] for c in range(8)], axis=0)
        out_ref[4 * n:4 * n + 4] = ordered.T.reshape(4, 32, 128)

    for copy, dz, dx in copies:
        pl.when(both(z_ok[dz], x_ok[dx]))(copy.wait_send)
    for copy, dy in y_copies:
        pl.when(y_ok[dy])(copy.wait_send)


def shards(planes, rims, noisy):
    return pl.pallas_call(
        kernel,
        out_shape=jax.ShapeDtypeStruct(noisy.shape, F32),
        in_specs=[pl.BlockSpec(memory_space=pl.ANY)] * 3,
        out_specs=pl.BlockSpec(memory_space=pltpu.VMEM),
        scratch_shapes=[
            pltpu.VMEM((26, PITCH, 128), F32),
            pltpu.VMEM((16, 4, 128), F32),
            pltpu.VMEM((16, 4, 128), F32),
            pltpu.VMEM((24, 4, 128), F32),
            pltpu.VMEM((24, 4, 128), F32),
            pltpu.VMEM((8, 4, 128), F32),
            pltpu.VMEM((8, 4, 128), F32),
            pltpu.VMEM((8, 4, 128), F32),
            pltpu.VMEM((8, 4, 128), F32),
            pltpu.VMEM((9, 8, 144, 128), F32),
            pltpu.VMEM((9, 8, 8, 128), F32),
            pltpu.VMEM((5, 512, 256), BF16),
            pltpu.VMEM((5, 2, 256, 256), BF16),
            pltpu.VMEM((432, 1024), BF16),
            pltpu.VMEM((2, 432, 512), F32),
            pltpu.VMEM((128, 512), F32),
            pltpu.VMEM((128, 512), F32),
            pltpu.SemaphoreType.DMA((3,)),
            pltpu.SemaphoreType.DMA((10,)),
            pltpu.SemaphoreType.DMA((10,)),
        ],
        compiler_params=pltpu.CompilerParams(collective_id=0, has_side_effects=True, vmem_limit_bytes=56 << 20),
    )(noisy, jnp.asarray(planes), jnp.asarray(rims))


def solution(mesh):
    planes, rims = box_tables()
    placed = P("gz", "gx", "gy")
    return jax.shard_map(
        functools.partial(shards, planes, rims), mesh=mesh, in_specs=(placed,), out_specs=placed, check_vma=False
    )
```

```python
import functools
import math

import jax
import jax.numpy as jnp
import ml_dtypes
import numpy as np
from jax import lax
from jax.experimental import pallas as pl
from jax.experimental.pallas import tpu as pltpu
from jax.sharding import PartitionSpec as P

GROUPS = ((0, 0), (0, 1), (1, -1), (1, 0), (1, 1))
VARIANTS = tuple((dz, dx) for dz in (-1, 0, 1) for dx in (-1, 0, 1))
SCALE = math.sqrt(math.log2(math.e) / 343.0)
SZ, SX, SY = 16, 32, 128
BASE, PITCH = 16, 64
MASKED = -1000.0
MESH = pl.DeviceIdType.MESH
F32, BF16 = jnp.float32, jnp.bfloat16


def box_tables():
    n = np.arange(256)
    k = np.arange(512)
    j = np.arange(256)
    zk, xk = k // 32, k % 32
    zj, s = j // 8, j % 8
    xj = np.where(s < 4, 32 + s, s - 8)
    planes, rims = [], []
    for dz, dx in GROUPS:
        xc = n % 32 - dx
        zc = 4 + n // 32 - dz
        near = (abs(zk[:, None] - zc) <= 3) & (abs(xk[:, None] - xc) <= 3)
        planes.append(-near.astype(np.float32))
        halves = []
        for half in range(2):
            near = (abs(zj[:, None] - zc - 8 * half) <= 3) & (abs(xj[:, None] - xc) <= 3) & (j < 192)[:, None]
            halves.append(-near.astype(np.float32))
        rims.append(np.stack(halves))
    return np.stack(planes).astype(ml_dtypes.bfloat16), np.stack(rims).astype(ml_dtypes.bfloat16)


def iota(shape, dim):
    return lax.broadcasted_iota(jnp.int32, shape, dim)


def kernel(x_ref, wp_hbm, wh_hbm, out_ref, ext, xs_lo, xs_hi, xp, xm, ys_lo, ys_hi, yp_lo, yp_hi, yx_lo, yx_hi,
           ye_lo, ye_hi, yr_lo, yr_hi, shifted, rows_h, wp, wh, lhs, dist, num, wsum, lhs_h, dist_h, edge, edge_p, ordered, local_sem, send_sem, recv_sem, ready):
    gx, gy, gz = lax.axis_index("gx"), lax.axis_index("gy"), lax.axis_index("gz")
    nx, ny, nz = lax.axis_size("gx"), lax.axis_size("gy"), lax.axis_size("gz")
    even = gy % 2 == 0
    odd_side = gy % 2 == 1

    def there(dz, dx, dy):
        ok = None
        for at, size, step in ((gz, nz, dz), (gx, nx, dx), (gy, ny, dy)):
            if step:
                inside = at > 0 if step < 0 else at < size - 1
                ok = inside if ok is None else jnp.logical_and(ok, inside)
        return ok

    def device(dz, dx, dy):
        return (gx + dx, gy + dy, gz + dz)

    around = [(dz, dx) for dz in (-1, 0, 1) for dx in (-1, 0, 1)]
    beside = [o for o in around if o != (0, 0)]
    barrier = pltpu.get_barrier_semaphore()
    for dy in (-1, 1):
        for dz, dx in around:
            @pl.when(jnp.logical_and(even, there(dz, dx, dy)))
            def _():
                pl.semaphore_signal(barrier, inc=1, device_id=device(dz, dx, dy), device_id_type=MESH)
    for dz, dx in beside:
        @pl.when(there(dz, dx, 0))
        def _():
            pl.semaphore_signal(barrier, inc=1, device_id=device(dz, dx, 0), device_id_type=MESH)

    def count(at, size):
        return (at > 0).astype(jnp.int32) + (at < size - 1).astype(jnp.int32)

    n_plane = (1 + count(gz, nz)) * (1 + count(gx, nx))
    n_beside = count(gy, ny)
    n_across = n_plane * n_beside

    own = pltpu.make_async_copy(x_ref, ext.at[pl.ds(4, SZ), pl.ds(BASE, SX), :], local_sem.at[0])
    own.start()
    tables = [pltpu.make_async_copy(wp_hbm, wp, local_sem.at[1]), pltpu.make_async_copy(wh_hbm, wh, local_sem.at[2])]

    send_z = {-1: pl.ds(0, 4), 0: pl.ds(0, 16), 1: pl.ds(12, 4)}
    land_z = {-1: pl.ds(20, 4), 0: pl.ds(4, 16), 1: pl.ds(0, 4)}

    def plane_parts(dz, dx):
        if dx == 0:
            return x_ref.at[send_z[dz]], ext.at[land_z[dz], pl.ds(BASE, SX), :]
        if dx == -1:
            return xs_lo.at[send_z[dz]], xp.at[land_z[dz]]
        return xs_hi.at[send_z[dz]], xm.at[land_z[dz]]

    def across_parts(dz, dx, dy):
        src, dst_p, dst_x = (ys_lo, yp_hi, yx_hi) if dy == -1 else (ys_hi, yp_lo, yx_lo)
        if dx == 0:
            tiles = {-1: pl.ds(0, 1), 0: pl.ds(0, 4), 1: pl.ds(3, 1)}[dz]
            land = {-1: pl.ds(5, 1), 0: pl.ds(1, 4), 1: pl.ds(0, 1)}[dz]
            return src.at[tiles], dst_p.at[land]
        return src.at[pl.ds(4, 1)], dst_x.at[pl.ds((0 if dx == -1 else 3) + 1 - dz, 1)]

    plane_copies, across_copies = [], []
    for dz, dx in beside:
        src, dst = plane_parts(dz, dx)
        i = len(plane_copies)
        copy = pltpu.make_async_remote_copy(
            src_ref=src, dst_ref=dst, send_sem=send_sem.at[i], recv_sem=recv_sem.at[i],
            device_id=device(dz, dx, 0), device_id_type=MESH)
        plane_copies.append((copy, dst, dz, dx, 0))
    for dy in (-1, 1):
        for dz, dx in [(0, 0)] + beside:
            src, dst = across_parts(dz, dx, dy)
            i = 8 + len(across_copies)
            copy = pltpu.make_async_remote_copy(
                src_ref=src, dst_ref=dst, send_sem=send_sem.at[i], recv_sem=recv_sem.at[i],
                device_id=device(dz, dx, dy), device_id_type=MESH)
            across_copies.append((copy, dst, dz, dx, dy))

    back_copies = []
    for i, (dy, src, dst) in enumerate(((-1, ye_lo, yr_hi), (1, ye_hi, yr_lo))):
        copy = pltpu.make_async_remote_copy(
            src_ref=src, dst_ref=dst, send_sem=send_sem.at[26 + i], recv_sem=recv_sem.at[26 + i],
            device_id=device(0, 0, dy), device_id_type=MESH)
        back_copies.append((copy, dst, 0, 0, dy))

    lane = iota((128, 128), 1)
    low_half = iota((8, 128), 0) < 4

    def block(v, k):
        dz, dx = VARIANTS[v]
        if k < 6:
            return jnp.concatenate([ext[4 * k + j + dz, BASE + dx:BASE + 32 + dx, :] for j in range(4)], axis=0)
        pieces = []
        for j in range(16 if k == 6 else 8):
            zi = 16 * (k - 6) + j + dz
            pieces.append(jnp.where(low_half, ext[zi, BASE + 32 + dx:BASE + 40 + dx, :], ext[zi, BASE - 8 + dx:BASE + dx, :]))
        if k == 7:
            pieces.append(jnp.zeros((64, 128), F32))
        return jnp.concatenate(pieces, axis=0)

    def place(v, k):
        turned = (block(v, k) * SCALE).T
        if k == 7 and v > 4:
            turned = jnp.where(lane == 64 + v - 4, 1.0, turned)
        for c in range(8):
            shifted[v, k, pl.ds(8 + c, 16, stride=8), :] = turned[16 * c:16 * c + 16]
        return turned

    pl.semaphore_wait(barrier, n_plane - 1 + n_across * odd_side.astype(jnp.int32))

    @pl.when(odd_side)
    def _():
        for dy in (-1, 1):
            @pl.when(there(0, 0, dy))
            def _():
                pl.semaphore_signal(ready, inc=1, device_id=device(0, 0, dy), device_id_type=MESH)

    own.wait()
    for k in range(1, 5):
        turned = place(4, k)
        ys_lo[k - 1] = ye_lo[k] = turned[0:4]
        ys_hi[k - 1] = ye_hi[k] = turned[124:128]
    rim = jnp.concatenate([jnp.where(low_half, ext[4 + j, BASE:BASE + 8, :], ext[4 + j, BASE + 24:BASE + 32, :]) for j in range(SZ)], axis=0)
    turned = (rim * SCALE).T
    ys_lo[4] = turned[0:4]
    ys_hi[4] = turned[124:128]

    @pl.when(odd_side)
    def _():
        for copy, dst, dz, dx, dy in across_copies:
            pl.when(there(dz, dx, dy))(copy.start)

    xs_lo[...] = ext[4:20, BASE:BASE + 4, :]
    xs_hi[...] = ext[4:20, BASE + 28:BASE + 32, :]
    for copy, dst, dz, dx, dy in plane_copies:
        pl.when(there(dz, dx, 0))(copy.start)
    for copy in tables:
        copy.start()

    ext[0:24, 0:BASE] = jnp.zeros((24, BASE, 128), F32)
    ext[0:24, BASE + SX:PITCH] = jnp.zeros((24, PITCH - BASE - SX, 128), F32)
    ext[24:26] = jnp.zeros((2, PITCH, 128), F32)
    for copy, dst, dz, dx, dy in plane_copies + across_copies + back_copies:
        @pl.when(jnp.logical_not(there(-dz, -dx, -dy)))
        def _():
            dst[...] = jnp.zeros(dst.shape, F32)

    early = [(v, k) for v, ks in ((7, range(1, 4)), (1, range(2, 5))) for k in ks]
    for v, k in early:
        place(v, k)

    for copy in tables:
        copy.wait()
    row = iota((16, 256), 0)
    col = iota((16, 256), 1)
    row_dz = jnp.where(row >= 2, 1, 0)
    row_dx = jnp.where(row == 1, 1, jnp.where((row >= 2) & (row < 5), row - 3, 0))
    known = (row >= 1) & (row < 5)
    for half in range(2):
        vz = gz * SZ + 8 * half + col // 32
        vx = gx * SX + col % 32

        def outside(sign):
            z, x = vz + sign * row_dz, vx + sign * row_dx
            return (z < 0) | (z >= nz * SZ) | (x < 0) | (x >= nx * SX)

        wh[0, half, 192:208, :] = jnp.where(known & outside(1), MASKED, 0.0).astype(BF16)
        back = known & outside(-1)
        for g in range(1, 5):
            wh[g, half, 192:208, :] = jnp.where(back & (row == g), MASKED, 0.0).astype(BF16)

    for copy, dst, dz, dx, dy in plane_copies:
        pl.when(there(-dz, -dx, 0))(copy.wait_recv)
    ext[0:24, BASE + 32:BASE + 36, :] = xp[...]
    ext[0:24, BASE - 4:BASE, :] = xm[...]
    for v in (4, 5, 6, 7, 8, 0, 1, 2, 3):
        for k in (range(8) if v >= 4 else range(1, 5)):
            if (v, k) not in early and not (v == 4 and 1 <= k <= 4):
                turned = place(v, k)
                if v == 4:
                    ye_lo[k] = turned[0:4]
                    ye_hi[k] = turned[124:128]

    z_step = gz // 2

    def answer(at_step):
        @pl.when(jnp.logical_and(even, jnp.minimum(z_step, 3) == at_step))
        def _():
            pl.semaphore_wait(ready, n_beside)
            for copy, dst, dz, dx, dy in back_copies:
                pl.when(there(0, 0, dy))(copy.start)

    lane8 = iota((8, 128), 1)
    sub = iota((8, 128), 0)

    def turn(value, by, axis):
        by = by % value.shape[axis]
        return value if by == 0 else pltpu.roll(value, by, axis)

    for v in range(9):
        for k in (range(8) if v >= 4 else range(1, 5)):
            shifted[v, k, 0:8, :] = turn(shifted[v, k, 128:136, :], 1, 0)
            shifted[v, k, 136:144, :] = turn(shifted[v, k, 8:16, :], -1, 0)

    def steps(g):
        return (1,) if g == 0 else (-1, 0, 1)

    def offset_index(g, d):
        return 0 if g == 0 else 3 * g - 2 + d

    def build(g):
        v = g + 4
        for d, dy in enumerate(steps(g)):
            for k in range(8):
                lanes = slice(128 * k, 128 * k + 128)
                error = None
                for j in range(8):
                    diff = shifted[4, k, 8 + 16 * j:24 + 16 * j, :] - shifted[v, k, 8 + 16 * j + 8 * dy:24 + 16 * j + 8 * dy, :]
                    square = diff * diff
                    if error is not None:
                        square = square + error
                    rounded = square.astype(BF16)
                    lhs[g % 2, 128 * d + 16 * j:128 * d + 16 * j + 16, lanes] = rounded
                    error = square - rounded.astype(F32)

    def multiply(g):
        rows = 128 * len(steps(g))
        for w, table in enumerate((0, g)):
            if w == 1 and g == 0:
                continue
            for half in range(2):
                total = jnp.dot(lhs[g % 2, 0:rows, 256 * half:256 * half + 512], wp[table], preferred_element_type=F32)
                total = total + jnp.dot(lhs[g % 2, 0:rows, 768:1024], wh[table, half], preferred_element_type=F32)
                for part in range(2):
                    dist[g % 2, w, 2 * half + part, 0:rows, :] = total[:, 128 * part:128 * part + 128]

    low4 = sub < 4

    def weights(g, w, d, dy, n, first):
        cache = {}

        def get(t):
            if t not in cache:
                if 0 <= t < 16:
                    value = dist[g % 2, w, n, 128 * d + 8 * t:128 * d + 8 * t + 8, :]
                    if t == 15 and dy == 1:
                        value = jnp.where(sub == 7, 0.0, value)
                    elif t == 0 and dy == -1:
                        value = jnp.where(sub == 0, 0.0, value)
                    cache[t] = value
                elif t < 0:
                    cache[t] = jnp.where(sub == 0, 0.0, turn(get(16 + t), 1, 0))
                else:
                    cache[t] = jnp.where(sub == 7, 0.0, turn(get(t - 16), -1, 0))
            return cache[t]

        total = get(first - 3)
        for t in range(first - 2, first + 4):
            total = total + get(t)
        result = []
        for i in range(16):
            if i:
                total = total + (get(first + i + 3) - get(first + i - 4))
            if i < 4 or i >= 12:
                at = 8 * (i if i < 4 else i - 8)
                edge[offset_index(g, d), w if g else (1 if first else 0), n, at:at + 8, :] = total
            result.append(jnp.exp2(total))
        return result

    def gather(g):
        v = g + 4
        for n in range(4):
            lanes = slice(128 * n, 128 * n + 128)
            for d, dy in enumerate(steps(g)):
                ahead = weights(g, 0, d, dy, n, 0)
                behind = weights(g, 1 if g else 0, d, dy, n, -dy)
                for t in range(16):
                    rows = slice(8 * t, 8 * t + 8)
                    up = shifted[v, n + 1, 8 + 8 * (t + dy):16 + 8 * (t + dy), :]
                    down = shifted[8 - v, n + 1, 8 + 8 * (t - dy):16 + 8 * (t - dy), :]
                    part = ahead[t] * up + behind[t] * down
                    part_w = ahead[t] + behind[t]
                    if g == 0:
                        num[rows, lanes] = part
                        wsum[rows, lanes] = part_w
                    else:
                        num[rows, lanes] += part
                        wsum[rows, lanes] += part_w

    for g in range(5):
        for at_step, at_group in ((3, 0), (2, 2), (1, 2), (0, 3)):
            if g == at_group:
                answer(at_step)
        build(g)
        multiply(g)
        gather(g)

    for v in range(9):
        for n in range(4):
            low = shifted[v, n + 1, pl.ds(8, 8, stride=8), :]
            high = shifted[v, n + 1, pl.ds(8 + 71, 8, stride=8), :]
            edge_p[v, n, 0] = jnp.where(low4, turn(low, 1, 0), turn(high, 1, 0))
            edge_p[v, n, 1] = jnp.where(low4, low, high)
            edge_p[v, n, 2] = jnp.where(low4, turn(low, -1, 0), turn(high, -1, 0))

    @pl.when(even)
    def _():
        for copy, dst, dz, dx, dy in across_copies:
            pl.when(there(-dz, -dx, -dy))(copy.wait_recv)
        for k in range(6):
            rows_h[4, k] = jnp.concatenate([yp_lo[k], yp_hi[k]], axis=0)
        from_rim = []
        for j in range(3):
            lower = jnp.concatenate([yx_lo[j], yx_hi[j]], axis=0)
            upper = jnp.concatenate([yx_lo[3 + j], yx_hi[3 + j]], axis=0)
            from_rim.append(jnp.where(lane8 % 8 < 4, lower, upper))
        rows_h[4, 6] = turn(jnp.where(lane8 >= 96, from_rim[0], from_rim[1]), 32, 1)
        rows_h[4, 7] = jnp.where(lane8 < 64, turn(jnp.where(lane8 >= 96, from_rim[1], from_rim[2]), 32, 1), 0.0)

    @pl.when(odd_side)
    def _():
        for copy, dst, dz, dx, dy in back_copies:
            pl.when(there(0, 0, -dy))(copy.wait_recv)
        for k in range(8):
            rows_h[4, k] = jnp.concatenate([yr_lo[k], yr_hi[k]], axis=0)

    for dx in (-1, 1):
        v = 4 + dx
        for k in range(6):
            value = turn(rows_h[4, k], -dx, 1)
            edge_lane = 31 if dx == 1 else 0
            source = rows_h[4, 6 + k // 4]
            for j in range(4):
                src_lane = (4 * (k % 4) + j) * 8 + (0 if dx == 1 else 7)
                dst_lane = 32 * j + edge_lane
                value = jnp.where(lane8 == dst_lane, turn(source, dst_lane - src_lane, 1), value)
            rows_h[v, k] = value
        for m in range(2):
            value = turn(rows_h[4, 6 + m], -dx, 1)
            for zz in range(16 if m == 0 else 8):
                k = 4 * m + zz // 4
                src_lane = 32 * (zz % 4) + (0 if dx == 1 else 31)
                dst_lane = 8 * zz + (7 if dx == 1 else 0)
                value = jnp.where(lane8 == dst_lane, turn(rows_h[4, k], dst_lane - src_lane, 1), value)
            rows_h[v, 6 + m] = value
    for dx in (-1, 0, 1):
        for k in range(6):
            here = turn(rows_h[4 + dx, k], -32, 1)
            after = turn(rows_h[4 + dx, k + 1], -32, 1) if k < 5 else here
            rows_h[7 + dx, k] = jnp.where(lane8 < 96, here, after)
            if 1 <= k <= 4:
                here = turn(rows_h[4 + dx, k], 32, 1)
                before = turn(rows_h[4 + dx, k - 1], 32, 1)
                rows_h[1 + dx, k] = jnp.where(lane8 >= 32, here, before)
        here, after = turn(rows_h[4 + dx, 6], -8, 1), turn(rows_h[4 + dx, 7], -8, 1)
        rows_h[7 + dx, 6] = jnp.where(lane8 < 120, here, after)
        rows_h[7 + dx, 7] = after
    for v in range(5, 9):
        rows_h[v, 7] = jnp.where(lane8 >= 64, jnp.where(lane8 == 64 + v - 4, 1.0, 0.0), rows_h[v, 7])

    for k in range(8):
        lanes = slice(128 * k, 128 * k + 128)

        def inner_low(v):
            first = turn(shifted[v, k, 8:16, :], 3, 0)
            return jnp.where(low4, jnp.where(sub == 3, first, turn(rows_h[v, k], -1, 0)), rows_h[v, k])

        def inner_high(v):
            last = turn(shifted[v, k, 128:136, :], -3, 0)
            return jnp.where(low4, rows_h[v, k], jnp.where(sub == 4, last, turn(rows_h[v, k], 1, 0)))

        base, base_low, base_high = rows_h[4, k], inner_low(4), inner_high(4)
        for g in range(5):
            v = g + 4
            if g:
                moved, moved_low, moved_high = rows_h[v, k], inner_low(v), inner_high(v)
            else:
                moved, moved_low, moved_high = base, base_low, base_high
            for d, dy in enumerate(steps(g)):
                if dy == 0:
                    diff = base - moved
                elif dy == 1:
                    diff = base_high - moved_low
                else:
                    diff = base_low - moved_high
                square = diff * diff
                high = square.astype(BF16).astype(F32)
                i = offset_index(g, d)
                lhs_h[16 * i:16 * i + 16, lanes] = jnp.concatenate([high, square - high], axis=0).astype(BF16)

    for g in range(5):
        first, rows = (0, 208) if g == 0 else (16 * offset_index(g, 0), 48)
        for half in range(2):
            total = jnp.dot(lhs_h[first:first + rows, 256 * half:256 * half + 512], wp[g], preferred_element_type=F32)
            total = total + jnp.dot(lhs_h[first:first + rows, 768:1024], wh[g, half], preferred_element_type=F32)
            for part in range(2):
                dist_h[1 if g else 0, 2 * half + part, first:first + rows, :] = total[:, 128 * part:128 * part + 128]

    keep_lo = jnp.where((sub == 0) & (gy == 0), 0.0, 1.0)
    keep_hi = jnp.where((sub == 7) & (gy == ny - 1), 0.0, 1.0)

    def edge_weights(i, w, dy, n, w_at):
        x = dist_h[w, n, 16 * i:16 * i + 8, :] + dist_h[w, n, 16 * i + 8:16 * i + 16, :]
        inward = jnp.where((sub == 3) | (sub == 4), 0.0, jnp.where(low4, turn(x, -1, 0), turn(x, 1, 0)))
        x = x + inward
        inward = jnp.where((sub >= 2) & (sub < 6), 0.0, jnp.where(low4, turn(x, -2, 0), turn(x, 2, 0)))
        x = x + inward
        fewer = jnp.where((sub == 3) | (sub == 4), 0.0, jnp.where(low4, turn(x, -1, 0), turn(x, 1, 0)))
        if dy == 0:
            halo = fewer
        elif (dy == 1) == (w_at == 0):
            halo = jnp.where(low4, fewer, x)
        else:
            halo = jnp.where(low4, x, fewer)
        low = edge[i, w_at, n, pl.ds(0, 4, stride=8), :]
        high = edge[i, w_at, n, pl.ds(39, 4, stride=8), :]
        return jnp.exp2(jnp.concatenate([low, high], axis=0) + halo)

    for n in range(4):
        def partner(v, dy):
            value = edge_p[v, n, 1 + dy]
            if dy == 1:
                return jnp.where(sub == 7, turn(rows_h[v, n + 1], 3, 0), value)
            if dy == -1:
                return jnp.where(sub == 0, turn(rows_h[v, n + 1], -3, 0), value)
            return value

        total, total_w = edge_p[4, n, 1], jnp.ones((8, 128), F32)
        for g in range(5):
            for d, dy in enumerate(steps(g)):
                i = offset_index(g, d)
                ahead = edge_weights(i, 0, dy, n, 0)
                behind = edge_weights(i, 1 if g else 0, dy, n, 1)
                if dy == 1:
                    ahead, behind = ahead * keep_hi, behind * keep_lo
                elif dy == -1:
                    ahead, behind = ahead * keep_lo, behind * keep_hi
                total = total + (ahead * partner(g + 4, dy) + behind * partner(4 - g, -dy))
                total_w = total_w + (ahead + behind)
        rim_rows = total * (1.0 / SCALE) / total_w

        lanes = slice(128 * n, 128 * n + 128)
        top = shifted[4, n + 1, 8:136, :] + num[:, lanes]
        ordered[n] = top * (1.0 / SCALE) / (1.0 + wsum[:, lanes])
        pieces = [ordered[n, pl.ds(c, 16, stride=8), :] for c in range(8)]
        pieces = [jnp.where(low4, rim_rows, pieces[0][0:8]), pieces[0][8:16]] + pieces[1:7] + [
            pieces[7][0:8], jnp.where(low4, pieces[7][8:16], rim_rows)]
        out_ref[4 * n:4 * n + 4] = jnp.concatenate(pieces, axis=0).T.reshape(4, 32, 128)

    for copy, dst, dz, dx, dy in plane_copies:
        pl.when(there(dz, dx, dy))(copy.wait_send)
    for side, sent in ((odd_side, across_copies), (even, back_copies)):
        for copy, dst, dz, dx, dy in sent:
            pl.when(jnp.logical_and(side, there(dz, dx, dy)))(copy.wait_send)


def shards(planes, rims, noisy):
    def vmem(*shape, dtype=F32):
        return pltpu.VMEM(shape, dtype)

    return pl.pallas_call(
        kernel,
        out_shape=jax.ShapeDtypeStruct(noisy.shape, F32),
        in_specs=[pl.BlockSpec(memory_space=pl.ANY)] * 3,
        out_specs=pl.BlockSpec(memory_space=pltpu.VMEM),
        scratch_shapes=[
            vmem(26, PITCH, 128),
            vmem(16, 4, 128), vmem(16, 4, 128), vmem(24, 4, 128), vmem(24, 4, 128),
            vmem(5, 4, 128), vmem(5, 4, 128),
            vmem(6, 4, 128), vmem(6, 4, 128), vmem(6, 4, 128), vmem(6, 4, 128),
            vmem(8, 4, 128), vmem(8, 4, 128), vmem(8, 4, 128), vmem(8, 4, 128),
            vmem(9, 8, 144, 128),
            vmem(9, 8, 8, 128),
            vmem(5, 512, 256, dtype=BF16), vmem(5, 2, 256, 256, dtype=BF16),
            vmem(2, 384, 1024, dtype=BF16), vmem(2, 2, 4, 384, 128),
            vmem(128, 512), vmem(128, 512),
            vmem(208, 1024, dtype=BF16), vmem(2, 4, 208, 128),
            vmem(13, 2, 4, 64, 128), vmem(9, 4, 3, 8, 128),
            vmem(4, 128, 128),
            pltpu.SemaphoreType.DMA((3,)),
            pltpu.SemaphoreType.DMA((28,)),
            pltpu.SemaphoreType.DMA((28,)),
            pltpu.SemaphoreType.REGULAR,
        ],
        compiler_params=pltpu.CompilerParams(collective_id=0, has_side_effects=True, vmem_limit_bytes=54848 << 10),
    )(noisy, jnp.asarray(planes), jnp.asarray(rims))


def solution(mesh):
    planes, rims = box_tables()
    placed = P("gz", "gx", "gy")
    return jax.shard_map(
        functools.partial(shards, planes, rims), mesh=mesh, in_specs=(placed,), out_specs=placed, check_vma=False
    )
```

```python
import functools
import math

import jax
import jax.numpy as jnp
import ml_dtypes
import numpy as np
from jax import lax
from jax.experimental import pallas as pl
from jax.experimental.pallas import tpu as pltpu
from jax.sharding import PartitionSpec as P

GROUPS = ((0, 0), (0, 1), (1, -1), (1, 0), (1, 1))
VARIANTS = tuple((dz, dx) for dz in (-1, 0, 1) for dx in (-1, 0, 1))
SCALE = math.sqrt(math.log2(math.e) / 343.0)
SZ, SX, SY = 16, 32, 128
BASE, PITCH = 16, 64
MASKED = -1000.0
ANSWER_AT = 2
MESH = pl.DeviceIdType.MESH
F32, BF16 = jnp.float32, jnp.bfloat16


def box_tables():
    n = np.arange(256)
    lane = np.arange(1024)
    rim = (lane < 128) | (lane >= 896)
    k, s = lane - 128, lane % 8
    zl = np.where(rim, lane % 128 // 8 + np.where(lane < 128, 0, 8), k // 32)
    xl = np.where(rim, np.where(s < 4, 32 + s, s - 8), k % 32)
    real = ~(rim & (lane % 128 >= 120))
    tables = []
    for dz, dx in GROUPS:
        halves = []
        for half in range(2):
            near = (abs(zl[:, None] - (4 + 8 * half + n // 32 - dz)) <= 3) & (abs(xl[:, None] - (n % 32 - dx)) <= 3)
            near = near & real[:, None]
            halves.append(-near[384 * half:384 * half + 640].astype(np.float32))
        tables.append(np.stack(halves))
    return np.stack(tables).astype(ml_dtypes.bfloat16)


def iota(shape, dim):
    return lax.broadcasted_iota(jnp.int32, shape, dim)


def kernel(x_ref, box_hbm, out_ref, ext, xs_lo, xs_hi, xp, xm, ys_lo, ys_hi, yp_lo, yp_hi, yx_lo, yx_hi, ye_lo, ye_hi, yr_lo, yr_hi,
           shifted, rows_h, box, lhs, dist, num, wsum, lhs_h, dist_h, edge, edge_p, ordered, local_sem, send_sem, recv_sem, ready):
    gx, gy, gz = lax.axis_index("gx"), lax.axis_index("gy"), lax.axis_index("gz")
    nx, ny, nz = lax.axis_size("gx"), lax.axis_size("gy"), lax.axis_size("gz")
    even = gy % 2 == 0
    odd_side = gy % 2 == 1

    def there(dz, dx, dy):
        ok = None
        for at, size, step in ((gz, nz, dz), (gx, nx, dx), (gy, ny, dy)):
            if step:
                inside = at > 0 if step < 0 else at < size - 1
                ok = inside if ok is None else jnp.logical_and(ok, inside)
        return ok

    def device(dz, dx, dy):
        return (gx + dx, gy + dy, gz + dz)

    around = [(dz, dx) for dz in (-1, 0, 1) for dx in (-1, 0, 1)]
    beside = [o for o in around if o != (0, 0)]
    barrier = pltpu.get_barrier_semaphore()
    direct_to = nz
    for dy in (-1, 1):
        for dz, dx in around:
            greets = jnp.logical_and(even, there(dz, dx, dy))
            if (dz, dx) != (0, 0):
                greets = jnp.logical_and(greets, gz < direct_to)

            @pl.when(greets)
            def _():
                pl.semaphore_signal(barrier, inc=1, device_id=device(dz, dx, dy), device_id_type=MESH)
    for dz, dx in beside:
        @pl.when(there(dz, dx, 0))
        def _():
            pl.semaphore_signal(barrier, inc=1, device_id=device(dz, dx, 0), device_id_type=MESH)

    def count(at, size):
        return (at > 0).astype(jnp.int32) + (at < size - 1).astype(jnp.int32)

    n_plane = (1 + count(gz, nz)) * (1 + count(gx, nx))
    n_beside = count(gy, ny)
    n_direct = sum(((gz + dz >= 0) & (gz + dz < direct_to)).astype(jnp.int32) for dz in (-1, 0, 1))
    n_across = n_beside * (n_direct * (1 + count(gx, nx)) + (gz >= direct_to).astype(jnp.int32))

    own = pltpu.make_async_copy(x_ref, ext.at[pl.ds(4, SZ), pl.ds(BASE, SX), :], local_sem.at[0])
    own.start()
    tables = [pltpu.make_async_copy(box_hbm, box, local_sem.at[1])]

    send_z = {-1: pl.ds(0, 4), 0: pl.ds(0, 16), 1: pl.ds(12, 4)}
    land_z = {-1: pl.ds(20, 4), 0: pl.ds(4, 16), 1: pl.ds(0, 4)}

    def plane_parts(dz, dx):
        if dx == 0:
            return ext.at[pl.ds(4 + send_z[dz].start, 4), pl.ds(BASE, SX), :], ext.at[land_z[dz], pl.ds(BASE, SX), :]
        if dx == -1:
            return xs_lo.at[send_z[dz]], xp.at[land_z[dz]]
        return xs_hi.at[send_z[dz]], xm.at[land_z[dz]]

    def across_parts(dz, dx, dy):
        src, dst_p, dst_x = (ys_lo, yp_hi, yx_hi) if dy == -1 else (ys_hi, yp_lo, yx_lo)
        if dx == 0:
            tiles = {-1: pl.ds(0, 1), 0: pl.ds(0, 4), 1: pl.ds(3, 1)}[dz]
            land = {-1: pl.ds(5, 1), 0: pl.ds(1, 4), 1: pl.ds(0, 1)}[dz]
            return src.at[tiles], dst_p.at[land]
        return src.at[pl.ds(4, 1)], dst_x.at[pl.ds((0 if dx == -1 else 3) + 1 - dz, 1)]

    plane_copies, across_copies = [], []
    for dz, dx in beside:
        src, dst = plane_parts(dz, dx)
        i = len(plane_copies)
        copy = pltpu.make_async_remote_copy(
            src_ref=src, dst_ref=dst, send_sem=send_sem.at[i], recv_sem=recv_sem.at[i],
            device_id=device(dz, dx, 0), device_id_type=MESH)
        plane_copies.append((copy, dst, dz, dx, 0))
    for dy in (-1, 1):
        for dz, dx in sorted(around, key=lambda o: -abs(o[0]) - abs(o[1])):
            src, dst = across_parts(dz, dx, dy)
            i = 10 + len(across_copies)
            copy = pltpu.make_async_remote_copy(
                src_ref=src, dst_ref=dst, send_sem=send_sem.at[i], recv_sem=recv_sem.at[i],
                device_id=device(dz, dx, dy), device_id_type=MESH)
            across_copies.append((copy, dst, dz, dx, dy))
    row_copies = []
    for i, (dy, src, dst) in enumerate(((-1, ye_lo, yr_hi), (1, ye_hi, yr_lo))):
        copy = pltpu.make_async_remote_copy(
            src_ref=src, dst_ref=dst, send_sem=send_sem.at[8 + i], recv_sem=recv_sem.at[8 + i],
            device_id=device(0, 0, dy), device_id_type=MESH)
        row_copies.append((copy, dst, 0, 0, dy))

    lane = iota((128, 128), 1)
    low_half = iota((8, 128), 0) < 4

    def block(v, k):
        dz, dx = VARIANTS[v]
        if k < 6:
            return jnp.concatenate([ext[4 * k + j + dz, BASE + dx:BASE + 32 + dx, :] for j in range(4)], axis=0)
        pieces = []
        for j in range(16):
            zi = 8 * (k - 6) + j + dz
            pieces.append(jnp.where(low_half, ext[zi, BASE + 32 + dx:BASE + 40 + dx, :], ext[zi, BASE - 8 + dx:BASE + dx, :]))
        return jnp.concatenate(pieces, axis=0)

    def place(v, k):
        whole = turned = (block(v, k) * SCALE).T
        if k >= 6:
            mark = jnp.where(lane == 120 + v - 4, 1.0, 0.0) if v > 4 else 0.0
            turned = jnp.where(lane >= 120, mark, turned)
        for c in range(8):
            shifted[v, k, pl.ds(8 + c, 16, stride=8), :] = turned[16 * c:16 * c + 16]
        return whole

    pl.semaphore_wait(barrier, n_plane - 1 + n_across * odd_side.astype(jnp.int32))

    @pl.when(odd_side)
    def _():
        for dy in (-1, 1):
            @pl.when(there(0, 0, dy))
            def _():
                pl.semaphore_signal(ready, inc=1, device_id=device(0, 0, dy), device_id_type=MESH)

    own.wait()
    def place_and_keep(v, k):
        turned = place(v, k)
        if v == 4:
            ye_lo[k] = turned[0:4]
            ye_hi[k] = turned[124:128]
            if 1 <= k <= 4:
                ys_lo[k - 1] = turned[0:4]
                ys_hi[k - 1] = turned[124:128]

    for k in range(1, 5):
        place_and_keep(4, k)
    rim = jnp.concatenate([jnp.where(low_half, ext[4 + j, BASE:BASE + 8, :], ext[4 + j, BASE + 24:BASE + 32, :]) for j in range(SZ)], axis=0)
    turned = (rim * SCALE).T
    ys_lo[4] = turned[0:4]
    ys_hi[4] = turned[124:128]

    def across_sent(dz, dx, dy):
        return jnp.logical_and(jnp.logical_and(odd_side, gz + dz < direct_to), there(dz, dx, dy))

    for copy, dst, dz, dx, dy in across_copies:
        pl.when(across_sent(dz, dx, dy))(copy.start)

    xs_lo[...] = ext[4:20, BASE:BASE + 4, :]
    xs_hi[...] = ext[4:20, BASE + 28:BASE + 32, :]
    for copy, dst, dz, dx, dy in plane_copies:
        pl.when(there(dz, dx, 0))(copy.start)
    for copy in tables:
        copy.start()

    ext[0:24, 0:BASE] = jnp.zeros((24, BASE, 128), F32)
    ext[0:24, BASE + SX:PITCH] = jnp.zeros((24, PITCH - BASE - SX, 128), F32)
    ext[24:26] = jnp.zeros((2, PITCH, 128), F32)
    for copy, dst, dz, dx, dy in plane_copies + row_copies + across_copies:
        @pl.when(jnp.logical_not(there(-dz, -dx, -dy)))
        def _():
            dst[...] = jnp.zeros(dst.shape, F32)

    early = [(v, k) for v, ks in ((7, range(1, 4)), (1, range(2, 5))) for k in ks]
    for v, k in early:
        place(v, k)

    for copy in tables:
        copy.wait()
    row = iota((16, 256), 0) - 8
    col = iota((16, 256), 1)
    row_dz = jnp.where(row >= 2, 1, 0)
    row_dx = jnp.where(row == 1, 1, jnp.where((row >= 2) & (row < 5), row - 3, 0))
    known = (row >= 1) & (row < 5)
    for half in range(2):
        vz = gz * SZ + 8 * half + col // 32
        vx = gx * SX + col % 32

        def outside(sign):
            z, x = vz + sign * row_dz, vx + sign * row_dx
            return (z < 0) | (z >= nz * SZ) | (x < 0) | (x >= nx * SX)

        mask_rows = slice(112 + 512 * half, 128 + 512 * half)
        box[0, half, mask_rows, :] = jnp.where(known & outside(1), MASKED, box[0, half, mask_rows, :].astype(F32)).astype(BF16)
        back = known & outside(-1)
        for g in range(1, 5):
            box[g, half, mask_rows, :] = jnp.where(back & (row == g), MASKED, box[g, half, mask_rows, :].astype(F32)).astype(BF16)

    for copy, dst, dz, dx, dy in plane_copies:
        pl.when(there(-dz, -dx, 0))(copy.wait_recv)
    ext[0:24, BASE + 32:BASE + 36, :] = xp[...]
    ext[0:24, BASE - 4:BASE, :] = xm[...]
    for k in range(8):
        if k < 1 or k > 4:
            place_and_keep(4, k)

    def send_rows():
        for copy, dst, dz, dx, dy in row_copies:
            pl.when(there(0, 0, dy))(copy.start)

    pl.when(jnp.logical_and(odd_side, gz >= direct_to))(send_rows)
    for v in (5, 6, 7, 8, 0, 1, 2, 3):
        for k in (range(8) if v > 4 else range(1, 5)):
            if (v, k) not in early:
                place(v, k)

    def answer():
        @pl.when(even)
        def _():
            pl.semaphore_wait(ready, n_beside)
            send_rows()

    lane8 = iota((8, 128), 1)
    sub = iota((8, 128), 0)

    def turn(value, by, axis):
        by = by % value.shape[axis]
        return value if by == 0 else pltpu.roll(value, by, axis)

    for v in range(9):
        for k in (range(8) if v >= 4 else range(1, 5)):
            shifted[v, k, 0:8, :] = turn(shifted[v, k, 128:136, :], 1, 0)
            shifted[v, k, 136:144, :] = turn(shifted[v, k, 8:16, :], -1, 0)

    def steps(g):
        return (1,) if g == 0 else (-1, 0, 1)

    def offset_index(g, d):
        return 0 if g == 0 else 3 * g - 2 + d

    def at_lanes(k):
        tile = k + 1 if k < 6 else 7 * (k - 6)
        return slice(128 * tile, 128 * tile + 128)

    def build(g, ks):
        v = g + 4
        for d, dy in enumerate(steps(g)):
            for k in ks:
                lanes = at_lanes(k)
                error = None
                for j in range(8):
                    diff = shifted[4, k, 8 + 16 * j:24 + 16 * j, :] - shifted[v, k, 8 + 16 * j + 8 * dy:24 + 16 * j + 8 * dy, :]
                    square = diff * diff
                    if error is not None:
                        square = square + error
                    rounded = square.astype(BF16)
                    lhs[g % 2, 128 * d + 16 * j:128 * d + 16 * j + 16, lanes] = rounded
                    error = square - rounded.astype(F32)

    def multiply(g, piece):
        rows = 128 * len(steps(g))
        half, w = piece // 2, piece % 2
        if w == 0 or g:
            table = g if w else 0
            total = jnp.dot(lhs[g % 2, 0:rows, 384 * half:384 * half + 640], box[table, half], preferred_element_type=F32)
            for part in range(2):
                dist[g % 2, w, 2 * half + part, 0:rows, :] = total[:, 128 * part:128 * part + 128]

    low4 = sub < 4

    def weights(g, w, d, dy, n, first):
        cache = {}

        def get(t):
            if t not in cache:
                if 0 <= t < 16:
                    value = dist[g % 2, w, n, 128 * d + 8 * t:128 * d + 8 * t + 8, :]
                    if t == 15 and dy == 1:
                        value = jnp.where(sub == 7, 0.0, value)
                    elif t == 0 and dy == -1:
                        value = jnp.where(sub == 0, 0.0, value)
                    cache[t] = value
                elif t < 0:
                    cache[t] = jnp.where(sub == 0, 0.0, turn(get(16 + t), 1, 0))
                else:
                    cache[t] = jnp.where(sub == 7, 0.0, turn(get(t - 16), -1, 0))
            return cache[t]

        total = get(first - 3)
        for t in range(first - 2, first + 4):
            total = total + get(t)
        result = []
        for i in range(16):
            if i:
                total = total + (get(first + i + 3) - get(first + i - 4))
            if i < 4 or i >= 12:
                at = 8 * (i if i < 4 else i - 8)
                edge[offset_index(g, d), w if g else (1 if first else 0), n, at:at + 8, :] = total
            result.append(jnp.exp2(total))
        return result

    def gather(g, ns):
        v = g + 4
        for n in ns:
            lanes = slice(128 * n, 128 * n + 128)
            for d, dy in enumerate(steps(g)):
                ahead = weights(g, 0, d, dy, n, 0)
                behind = weights(g, 1 if g else 0, d, dy, n, -dy)
                for t in range(16):
                    rows = slice(8 * t, 8 * t + 8)
                    up = shifted[v, n + 1, 8 + 8 * (t + dy):16 + 8 * (t + dy), :]
                    down = shifted[8 - v, n + 1, 8 + 8 * (t - dy):16 + 8 * (t - dy), :]
                    part = ahead[t] * up + behind[t] * down
                    part_w = ahead[t] + behind[t]
                    if g == 0:
                        num[rows, lanes] = part
                        wsum[rows, lanes] = part_w
                    else:
                        num[rows, lanes] += part
                        wsum[rows, lanes] += part_w

    build(0, range(8))
    for g in range(6):
        if g == ANSWER_AT:
            answer()
        for piece in range(4):
            if g < 5:
                multiply(g, piece)
            if g < 4:
                build(g + 1, (2 * piece, 2 * piece + 1))
            if g > 0:
                gather(g - 1, (piece,))

    for v in range(9):
        for n in range(4):
            low = shifted[v, n + 1, pl.ds(8, 8, stride=8), :]
            high = shifted[v, n + 1, pl.ds(8 + 71, 8, stride=8), :]
            edge_p[v, n, 0] = jnp.where(low4, turn(low, 1, 0), turn(high, 1, 0))
            edge_p[v, n, 1] = jnp.where(low4, low, high)
            edge_p[v, n, 2] = jnp.where(low4, turn(low, -1, 0), turn(high, -1, 0))

    got_across = jnp.logical_and(even, gz < direct_to)

    @pl.when(got_across)
    def _():
        for copy, dst, dz, dx, dy in across_copies:
            pl.when(there(-dz, -dx, -dy))(copy.wait_recv)
        for k in range(6):
            rows_h[4, k] = jnp.concatenate([yp_lo[k], yp_hi[k]], axis=0)
        from_rim = []
        for j in range(3):
            lower = jnp.concatenate([yx_lo[j], yx_hi[j]], axis=0)
            upper = jnp.concatenate([yx_lo[3 + j], yx_hi[3 + j]], axis=0)
            from_rim.append(jnp.where(lane8 % 8 < 4, lower, upper))
        rows_h[4, 6] = turn(jnp.where(lane8 >= 96, from_rim[0], from_rim[1]), 32, 1)
        rows_h[4, 7] = turn(jnp.where(lane8 >= 32, from_rim[1], from_rim[2]), -32, 1)

    @pl.when(jnp.logical_not(got_across))
    def _():
        for copy, dst, dz, dx, dy in row_copies:
            pl.when(there(0, 0, -dy))(copy.wait_recv)
        for k in range(8):
            rows_h[4, k] = jnp.concatenate([yr_lo[k], yr_hi[k]], axis=0)

    for dx in (-1, 1):
        v = 4 + dx
        for k in range(6):
            value = turn(rows_h[4, k], -dx, 1)
            edge_lane = 31 if dx == 1 else 0
            source = rows_h[4, 6 + k // 4]
            first_z = 4 * k - 8 * (k // 4)
            for j in range(4):
                src_lane = (first_z + j) * 8 + (0 if dx == 1 else 7)
                dst_lane = 32 * j + edge_lane
                value = jnp.where(lane8 == dst_lane, turn(source, dst_lane - src_lane, 1), value)
            rows_h[v, k] = value
        for m in range(2):
            value = turn(rows_h[4, 6 + m], -dx, 1)
            for zz in range(16):
                k = 2 * m + zz // 4
                src_lane = 32 * (zz % 4) + (0 if dx == 1 else 31)
                dst_lane = 8 * zz + (7 if dx == 1 else 0)
                value = jnp.where(lane8 == dst_lane, turn(rows_h[4, k], dst_lane - src_lane, 1), value)
            rows_h[v, 6 + m] = value
    for dx in (-1, 0, 1):
        for k in range(6):
            here = turn(rows_h[4 + dx, k], -32, 1)
            after = turn(rows_h[4 + dx, k + 1], -32, 1) if k < 5 else here
            rows_h[7 + dx, k] = jnp.where(lane8 < 96, here, after)
            if 1 <= k <= 4:
                here = turn(rows_h[4 + dx, k], 32, 1)
                before = turn(rows_h[4 + dx, k - 1], 32, 1)
                rows_h[1 + dx, k] = jnp.where(lane8 >= 32, here, before)
        for m in range(2):
            rows_h[7 + dx, 6 + m] = turn(rows_h[4 + dx, 6 + m], -8, 1)
    for v in range(4, 9):
        mark = jnp.where(lane8 == 120 + v - 4, 1.0, 0.0) if v > 4 else 0.0
        for m in range(2):
            rows_h[v, 6 + m] = jnp.where(lane8 >= 120, mark, rows_h[v, 6 + m])

    for k in range(8):
        lanes = at_lanes(k)

        def inner_low(v):
            first = turn(shifted[v, k, 8:16, :], 3, 0)
            return jnp.where(low4, jnp.where(sub == 3, first, turn(rows_h[v, k], -1, 0)), rows_h[v, k])

        def inner_high(v):
            last = turn(shifted[v, k, 128:136, :], -3, 0)
            return jnp.where(low4, rows_h[v, k], jnp.where(sub == 4, last, turn(rows_h[v, k], 1, 0)))

        base, base_low, base_high = rows_h[4, k], inner_low(4), inner_high(4)
        for g in range(5):
            v = g + 4
            if g:
                moved, moved_low, moved_high = rows_h[v, k], inner_low(v), inner_high(v)
            else:
                moved, moved_low, moved_high = base, base_low, base_high
            for d, dy in enumerate(steps(g)):
                if dy == 0:
                    diff = base - moved
                elif dy == 1:
                    diff = base_high - moved_low
                else:
                    diff = base_low - moved_high
                square = diff * diff
                high = square.astype(BF16).astype(F32)
                i = offset_index(g, d)
                lhs_h[16 * i:16 * i + 16, lanes] = jnp.concatenate([high, square - high], axis=0).astype(BF16)

    for g in range(5):
        first, rows = (0, 208) if g == 0 else (16 * offset_index(g, 0), 48)
        for half in range(2):
            total = jnp.dot(lhs_h[first:first + rows, 384 * half:384 * half + 640], box[g, half], preferred_element_type=F32)
            for part in range(2):
                dist_h[1 if g else 0, 2 * half + part, first:first + rows, :] = total[:, 128 * part:128 * part + 128]

    keep_lo = jnp.where((sub == 0) & (gy == 0), 0.0, 1.0)
    keep_hi = jnp.where((sub == 7) & (gy == ny - 1), 0.0, 1.0)

    def edge_weights(i, w, dy, n, w_at):
        x = dist_h[w, n, 16 * i:16 * i + 8, :] + dist_h[w, n, 16 * i + 8:16 * i + 16, :]
        inward = jnp.where((sub == 3) | (sub == 4), 0.0, jnp.where(low4, turn(x, -1, 0), turn(x, 1, 0)))
        x = x + inward
        inward = jnp.where((sub >= 2) & (sub < 6), 0.0, jnp.where(low4, turn(x, -2, 0), turn(x, 2, 0)))
        x = x + inward
        fewer = jnp.where((sub == 3) | (sub == 4), 0.0, jnp.where(low4, turn(x, -1, 0), turn(x, 1, 0)))
        if dy == 0:
            halo = fewer
        elif (dy == 1) == (w_at == 0):
            halo = jnp.where(low4, fewer, x)
        else:
            halo = jnp.where(low4, x, fewer)
        low = edge[i, w_at, n, pl.ds(0, 4, stride=8), :]
        high = edge[i, w_at, n, pl.ds(39, 4, stride=8), :]
        return jnp.exp2(jnp.concatenate([low, high], axis=0) + halo)

    for n in range(4):
        def partner(v, dy):
            value = edge_p[v, n, 1 + dy]
            if dy == 1:
                return jnp.where(sub == 7, turn(rows_h[v, n + 1], 3, 0), value)
            if dy == -1:
                return jnp.where(sub == 0, turn(rows_h[v, n + 1], -3, 0), value)
            return value

        total, total_w = edge_p[4, n, 1], jnp.ones((8, 128), F32)
        for g in range(5):
            for d, dy in enumerate(steps(g)):
                i = offset_index(g, d)
                ahead = edge_weights(i, 0, dy, n, 0)
                behind = edge_weights(i, 1 if g else 0, dy, n, 1)
                if dy == 1:
                    ahead, behind = ahead * keep_hi, behind * keep_lo
                elif dy == -1:
                    ahead, behind = ahead * keep_lo, behind * keep_hi
                total = total + (ahead * partner(g + 4, dy) + behind * partner(4 - g, -dy))
                total_w = total_w + (ahead + behind)
        rim_rows = total * (1.0 / SCALE) / total_w

        lanes = slice(128 * n, 128 * n + 128)
        top = shifted[4, n + 1, 8:136, :] + num[:, lanes]
        ordered[n] = top * (1.0 / SCALE) / (1.0 + wsum[:, lanes])
        pieces = [ordered[n, pl.ds(c, 16, stride=8), :] for c in range(8)]
        pieces = [jnp.where(low4, rim_rows, pieces[0][0:8]), pieces[0][8:16]] + pieces[1:7] + [
            pieces[7][0:8], jnp.where(low4, pieces[7][8:16], rim_rows)]
        out_ref[4 * n:4 * n + 4] = jnp.concatenate(pieces, axis=0).T.reshape(4, 32, 128)

    for copy, dst, dz, dx, dy in plane_copies:
        pl.when(there(dz, dx, dy))(copy.wait_send)
    for copy, dst, dz, dx, dy in across_copies:
        pl.when(across_sent(dz, dx, dy))(copy.wait_send)
    for copy, dst, dz, dx, dy in row_copies:
        pl.when(jnp.logical_and(there(dz, dx, dy), jnp.logical_or(even, gz >= direct_to)))(copy.wait_send)


def shards(tables, noisy):
    def vmem(*shape, dtype=F32):
        return pltpu.VMEM(shape, dtype)

    return pl.pallas_call(
        kernel,
        out_shape=jax.ShapeDtypeStruct(noisy.shape, F32),
        in_specs=[pl.BlockSpec(memory_space=pl.ANY)] * 2,
        out_specs=pl.BlockSpec(memory_space=pltpu.VMEM),
        scratch_shapes=[
            vmem(26, PITCH, 128),
            vmem(16, 4, 128), vmem(16, 4, 128), vmem(24, 4, 128), vmem(24, 4, 128),
            vmem(5, 4, 128), vmem(5, 4, 128),
            vmem(6, 4, 128), vmem(6, 4, 128), vmem(6, 4, 128), vmem(6, 4, 128),
            vmem(8, 4, 128), vmem(8, 4, 128), vmem(8, 4, 128), vmem(8, 4, 128),
            vmem(9, 8, 144, 128),
            vmem(9, 8, 8, 128),
            vmem(5, 2, 640, 256, dtype=BF16),
            vmem(2, 384, 1024, dtype=BF16), vmem(2, 2, 4, 384, 128),
            vmem(128, 512), vmem(128, 512),
            vmem(208, 1024, dtype=BF16), vmem(2, 4, 208, 128),
            vmem(13, 2, 4, 64, 128), vmem(9, 4, 3, 8, 128),
            vmem(4, 128, 128),
            pltpu.SemaphoreType.DMA((2,)),
            pltpu.SemaphoreType.DMA((28,)),
            pltpu.SemaphoreType.DMA((28,)),
            pltpu.SemaphoreType.REGULAR,
        ],
        compiler_params=pltpu.CompilerParams(collective_id=0, has_side_effects=True, vmem_limit_bytes=54848 << 10),
    )(noisy, jnp.asarray(tables))


def solution(mesh):
    placed = P("gz", "gx", "gy")
    return jax.shard_map(
        functools.partial(shards, box_tables()), mesh=mesh, in_specs=(placed,), out_specs=placed, check_vma=False
    )
```

```python
import functools
import math

import jax
import jax.numpy as jnp
import ml_dtypes
import numpy as np
from jax import lax
from jax.experimental import pallas as pl
from jax.experimental.pallas import tpu as pltpu
from jax.sharding import PartitionSpec as P

GROUPS = ((0, 0), (0, 1), (1, -1), (1, 0), (1, 1))
VARIANTS = tuple((dz, dx) for dz in (-1, 0, 1) for dx in (-1, 0, 1))
SCALE = math.sqrt(math.log2(math.e) / 343.0)
SZ, SX, SY = 16, 32, 128
BASE, PITCH = 16, 64
MASKED = -1000.0
ANSWER_AT, ANSWER_LATE, LATE_BELOW = 2, 4, 2
ROWS_FIRST_BELOW = 3
MESH = pl.DeviceIdType.MESH
F32, BF16 = jnp.float32, jnp.bfloat16


def box_tables():
    n = np.arange(256)
    lane = np.arange(1024)
    rim = (lane < 128) | (lane >= 896)
    k, s = lane - 128, lane % 8
    zl = np.where(rim, lane % 128 // 8 + np.where(lane < 128, 0, 8), k // 32)
    xl = np.where(rim, np.where(s < 4, 32 + s, s - 8), k % 32)
    real = ~(rim & (lane % 128 >= 120))
    tables = []
    for dz, dx in GROUPS:
        halves = []
        for half in range(2):
            near = (abs(zl[:, None] - (4 + 8 * half + n // 32 - dz)) <= 3) & (abs(xl[:, None] - (n % 32 - dx)) <= 3)
            near = near & real[:, None]
            halves.append(-near[384 * half:384 * half + 640].astype(np.float32))
        tables.append(np.stack(halves))
    return np.stack(tables).astype(ml_dtypes.bfloat16)


def iota(shape, dim):
    return lax.broadcasted_iota(jnp.int32, shape, dim)


def kernel(x_ref, box_hbm, out_ref, ext, xs_lo, xs_hi, xp, xm, ys_lo, ys_hi, yp_lo, yp_hi, yx_lo, yx_hi, ye_lo, ye_hi, yr_lo, yr_hi,
           shifted, rows_h, box, lhs, dist, num, wsum, lhs_h, dist_h, edge, edge_sum, edge_p, ordered, local_sem, send_sem, recv_sem, ready):
    gx, gy, gz = lax.axis_index("gx"), lax.axis_index("gy"), lax.axis_index("gz")
    nx, ny, nz = lax.axis_size("gx"), lax.axis_size("gy"), lax.axis_size("gz")
    even = gy % 2 == 0
    odd_side = gy % 2 == 1

    def there(dz, dx, dy):
        ok = None
        for at, size, step in ((gz, nz, dz), (gx, nx, dx), (gy, ny, dy)):
            if step:
                inside = at > 0 if step < 0 else at < size - 1
                ok = inside if ok is None else jnp.logical_and(ok, inside)
        return ok

    def device(dz, dx, dy):
        return (gx + dx, gy + dy, gz + dz)

    around = [(dz, dx) for dz in (-1, 0, 1) for dx in (-1, 0, 1)]
    beside = [o for o in around if o != (0, 0)]
    barrier = pltpu.get_barrier_semaphore()
    direct_to = nz - 2
    for dy in (-1, 1):
        for dz, dx in around:
            greets = jnp.logical_and(even, there(dz, dx, dy))
            if (dz, dx) != (0, 0):
                greets = jnp.logical_and(greets, gz < direct_to)

            @pl.when(greets)
            def _():
                pl.semaphore_signal(barrier, inc=1, device_id=device(dz, dx, dy), device_id_type=MESH)
    for dz, dx in beside:
        @pl.when(there(dz, dx, 0))
        def _():
            pl.semaphore_signal(barrier, inc=1, device_id=device(dz, dx, 0), device_id_type=MESH)

    def count(at, size):
        return (at > 0).astype(jnp.int32) + (at < size - 1).astype(jnp.int32)

    n_plane = (1 + count(gz, nz)) * (1 + count(gx, nx))
    n_beside = count(gy, ny)
    n_direct = sum(((gz + dz >= 0) & (gz + dz < direct_to)).astype(jnp.int32) for dz in (-1, 0, 1))
    n_across = n_beside * (n_direct * (1 + count(gx, nx)) + (gz >= direct_to).astype(jnp.int32))

    own = pltpu.make_async_copy(x_ref, ext.at[pl.ds(4, SZ), pl.ds(BASE, SX), :], local_sem.at[0])
    own.start()
    tables = [pltpu.make_async_copy(box_hbm, box, local_sem.at[1])]

    send_z = {-1: pl.ds(0, 4), 0: pl.ds(0, 16), 1: pl.ds(12, 4)}
    land_z = {-1: pl.ds(20, 4), 0: pl.ds(4, 16), 1: pl.ds(0, 4)}

    def plane_parts(dz, dx):
        if dx == 0:
            return ext.at[pl.ds(4 + send_z[dz].start, 4), pl.ds(BASE, SX), :], ext.at[land_z[dz], pl.ds(BASE, SX), :]
        if dx == -1:
            return xs_lo.at[send_z[dz]], xp.at[land_z[dz]]
        return xs_hi.at[send_z[dz]], xm.at[land_z[dz]]

    def across_parts(dz, dx, dy):
        src, dst_p, dst_x = (ys_lo, yp_hi, yx_hi) if dy == -1 else (ys_hi, yp_lo, yx_lo)
        if dx == 0:
            tiles = {-1: pl.ds(0, 1), 0: pl.ds(0, 4), 1: pl.ds(3, 1)}[dz]
            land = {-1: pl.ds(5, 1), 0: pl.ds(1, 4), 1: pl.ds(0, 1)}[dz]
            return src.at[tiles], dst_p.at[land]
        return src.at[pl.ds(4, 1)], dst_x.at[pl.ds((0 if dx == -1 else 3) + 1 - dz, 1)]

    plane_copies, across_copies = [], []
    for dz, dx in beside:
        src, dst = plane_parts(dz, dx)
        i = len(plane_copies)
        copy = pltpu.make_async_remote_copy(
            src_ref=src, dst_ref=dst, send_sem=send_sem.at[i], recv_sem=recv_sem.at[i],
            device_id=device(dz, dx, 0), device_id_type=MESH)
        plane_copies.append((copy, dst, dz, dx, 0))
    for dy in (-1, 1):
        for dz, dx in sorted(around, key=lambda o: -abs(o[0]) - abs(o[1])):
            src, dst = across_parts(dz, dx, dy)
            i = 10 + len(across_copies)
            copy = pltpu.make_async_remote_copy(
                src_ref=src, dst_ref=dst, send_sem=send_sem.at[i], recv_sem=recv_sem.at[i],
                device_id=device(dz, dx, dy), device_id_type=MESH)
            across_copies.append((copy, dst, dz, dx, dy))
    row_copies = []
    for i, (dy, src, dst) in enumerate(((-1, ye_lo, yr_hi), (1, ye_hi, yr_lo))):
        copy = pltpu.make_async_remote_copy(
            src_ref=src, dst_ref=dst, send_sem=send_sem.at[8 + i], recv_sem=recv_sem.at[8 + i],
            device_id=device(0, 0, dy), device_id_type=MESH)
        row_copies.append((copy, dst, 0, 0, dy))

    lane = iota((128, 128), 1)
    low_half = iota((8, 128), 0) < 4

    def block(v, k):
        dz, dx = VARIANTS[v]
        if k < 6:
            return jnp.concatenate([ext[4 * k + j + dz, BASE + dx:BASE + 32 + dx, :] for j in range(4)], axis=0)
        pieces = []
        for j in range(16):
            zi = 8 * (k - 6) + j + dz
            pieces.append(jnp.where(low_half, ext[zi, BASE + 32 + dx:BASE + 40 + dx, :], ext[zi, BASE - 8 + dx:BASE + dx, :]))
        return jnp.concatenate(pieces, axis=0)

    def place(v, k):
        whole = turned = (block(v, k) * SCALE).T
        if k >= 6:
            mark = jnp.where(lane == 120 + v - 4, 1.0, 0.0) if v > 4 else 0.0
            turned = jnp.where(lane >= 120, mark, turned)
        for c in range(8):
            shifted[v, k, pl.ds(8 + c, 16, stride=8), :] = turned[16 * c:16 * c + 16]
        return whole

    pl.semaphore_wait(barrier, n_plane - 1 + n_across * odd_side.astype(jnp.int32))

    @pl.when(odd_side)
    def _():
        for dy in (-1, 1):
            @pl.when(there(0, 0, dy))
            def _():
                pl.semaphore_signal(ready, inc=1, device_id=device(0, 0, dy), device_id_type=MESH)

    own.wait()
    xs_lo[...] = ext[4:20, BASE:BASE + 4, :]
    xs_hi[...] = ext[4:20, BASE + 28:BASE + 32, :]
    rows_first = jnp.logical_and(odd_side, gz < ROWS_FIRST_BELOW)

    def send_planes():
        for copy, dst, dz, dx, dy in plane_copies:
            pl.when(there(dz, dx, 0))(copy.start)

    pl.when(jnp.logical_not(rows_first))(send_planes)
    for copy in tables:
        copy.start()
    def place_and_keep(v, k):
        turned = place(v, k)
        if v == 4:
            ye_lo[k] = turned[0:4]
            ye_hi[k] = turned[124:128]
            if 1 <= k <= 4:
                ys_lo[k - 1] = turned[0:4]
                ys_hi[k - 1] = turned[124:128]

    for k in range(1, 5):
        place_and_keep(4, k)
    rim = jnp.concatenate([jnp.where(low_half, ext[4 + j, BASE:BASE + 8, :], ext[4 + j, BASE + 24:BASE + 32, :]) for j in range(SZ)], axis=0)
    turned = (rim * SCALE).T
    ys_lo[4] = turned[0:4]
    ys_hi[4] = turned[124:128]

    def across_sent(dz, dx, dy):
        return jnp.logical_and(jnp.logical_and(odd_side, gz + dz < direct_to), there(dz, dx, dy))

    for copy, dst, dz, dx, dy in across_copies:
        pl.when(across_sent(dz, dx, dy))(copy.start)

    pl.when(rows_first)(send_planes)
    ext[0:24, 0:BASE] = jnp.zeros((24, BASE, 128), F32)
    ext[0:24, BASE + SX:PITCH] = jnp.zeros((24, PITCH - BASE - SX, 128), F32)
    ext[24:26] = jnp.zeros((2, PITCH, 128), F32)
    for copy, dst, dz, dx, dy in plane_copies + row_copies + across_copies:
        @pl.when(jnp.logical_not(there(-dz, -dx, -dy)))
        def _():
            dst[...] = jnp.zeros(dst.shape, F32)

    early = [(v, k) for v, ks in ((7, range(1, 4)), (1, range(2, 5))) for k in ks]
    for v, k in early:
        place(v, k)

    for copy in tables:
        copy.wait()
    row = iota((16, 256), 0) - 8
    col = iota((16, 256), 1)
    row_dz = jnp.where(row >= 2, 1, 0)
    row_dx = jnp.where(row == 1, 1, jnp.where((row >= 2) & (row < 5), row - 3, 0))
    known = (row >= 1) & (row < 5)
    for half in range(2):
        vz = gz * SZ + 8 * half + col // 32
        vx = gx * SX + col % 32

        def outside(sign):
            z, x = vz + sign * row_dz, vx + sign * row_dx
            return (z < 0) | (z >= nz * SZ) | (x < 0) | (x >= nx * SX)

        mask_rows = slice(112 + 512 * half, 128 + 512 * half)
        box[0, half, mask_rows, :] = jnp.where(known & outside(1), MASKED, box[0, half, mask_rows, :].astype(F32)).astype(BF16)
        back = known & outside(-1)
        for g in range(1, 5):
            box[g, half, mask_rows, :] = jnp.where(back & (row == g), MASKED, box[g, half, mask_rows, :].astype(F32)).astype(BF16)

    for copy, dst, dz, dx, dy in plane_copies:
        pl.when(there(-dz, -dx, 0))(copy.wait_recv)
    ext[0:24, BASE + 32:BASE + 36, :] = xp[...]
    ext[0:24, BASE - 4:BASE, :] = xm[...]
    for k in range(8):
        if k < 1 or k > 4:
            place_and_keep(4, k)

    def send_rows():
        for copy, dst, dz, dx, dy in row_copies:
            pl.when(there(0, 0, dy))(copy.start)

    pl.when(jnp.logical_and(odd_side, gz >= direct_to))(send_rows)
    for v in (5, 6, 7, 8, 0, 1, 2, 3):
        for k in (range(8) if v > 4 else range(1, 5)):
            if (v, k) not in early:
                place(v, k)

    def answer(here):
        @pl.when(jnp.logical_and(even, here))
        def _():
            pl.semaphore_wait(ready, n_beside)
            send_rows()

    lane8 = iota((8, 128), 1)
    sub = iota((8, 128), 0)

    def turn(value, by, axis):
        by = by % value.shape[axis]
        return value if by == 0 else pltpu.roll(value, by, axis)

    for v in range(9):
        for k in (range(8) if v >= 4 else range(1, 5)):
            shifted[v, k, 0:8, :] = turn(shifted[v, k, 128:136, :], 1, 0)
            shifted[v, k, 136:144, :] = turn(shifted[v, k, 8:16, :], -1, 0)

    def steps(g):
        return (1,) if g == 0 else (-1, 0, 1)

    def offset_index(g, d):
        return 0 if g == 0 else 3 * g - 2 + d

    def at_lanes(k):
        tile = k + 1 if k < 6 else 7 * (k - 6)
        return slice(128 * tile, 128 * tile + 128)

    def build(g, ks):
        v = g + 4
        for d, dy in enumerate(steps(g)):
            for k in ks:
                lanes = at_lanes(k)
                error = None
                for j in range(8):
                    diff = shifted[4, k, 8 + 16 * j:24 + 16 * j, :] - shifted[v, k, 8 + 16 * j + 8 * dy:24 + 16 * j + 8 * dy, :]
                    square = diff * diff
                    if error is not None:
                        square = square + error
                    rounded = square.astype(BF16)
                    lhs[g % 2, 128 * d + 16 * j:128 * d + 16 * j + 16, lanes] = rounded
                    error = square - rounded.astype(F32)

    def multiply(g, piece):
        rows = 128 * len(steps(g))
        half, w = piece // 2, piece % 2
        if w == 0 or g:
            table = g if w else 0
            total = jnp.dot(lhs[g % 2, 0:rows, 384 * half:384 * half + 640], box[table, half], preferred_element_type=F32)
            for part in range(2):
                dist[g % 2, w, 2 * half + part, 0:rows, :] = total[:, 128 * part:128 * part + 128]

    low4 = sub < 4

    def weights(g, w, d, dy, n, first):
        cache = {}

        def get(t):
            if t not in cache:
                if 0 <= t < 16:
                    value = dist[g % 2, w, n, 128 * d + 8 * t:128 * d + 8 * t + 8, :]
                    if t == 15 and dy == 1:
                        value = jnp.where(sub == 7, 0.0, value)
                    elif t == 0 and dy == -1:
                        value = jnp.where(sub == 0, 0.0, value)
                    cache[t] = value
                elif t < 0:
                    cache[t] = jnp.where(sub == 0, 0.0, turn(get(16 + t), 1, 0))
                else:
                    cache[t] = jnp.where(sub == 7, 0.0, turn(get(t - 16), -1, 0))
            return cache[t]

        total = get(first - 3)
        for t in range(first - 2, first + 4):
            total = total + get(t)
        result = []
        for i in range(16):
            if i:
                total = total + (get(first + i + 3) - get(first + i - 4))
            if i < 4 or i >= 12:
                at = 8 * (i if i < 4 else i - 8)
                edge[offset_index(g, d), w if g else (1 if first else 0), n, at:at + 8, :] = total
            result.append(jnp.exp2(total))
        return result

    def gather(g, ns):
        v = g + 4
        for n in ns:
            lanes = slice(128 * n, 128 * n + 128)
            for d, dy in enumerate(steps(g)):
                ahead = weights(g, 0, d, dy, n, 0)
                behind = weights(g, 1 if g else 0, d, dy, n, -dy)
                for t in range(16):
                    rows = slice(8 * t, 8 * t + 8)
                    up = shifted[v, n + 1, 8 + 8 * (t + dy):16 + 8 * (t + dy), :]
                    down = shifted[8 - v, n + 1, 8 + 8 * (t - dy):16 + 8 * (t - dy), :]
                    part = ahead[t] * up + behind[t] * down
                    part_w = ahead[t] + behind[t]
                    if g == 0:
                        num[rows, lanes] = part
                        wsum[rows, lanes] = part_w
                    else:
                        num[rows, lanes] += part
                        wsum[rows, lanes] += part_w

    build(0, range(8))
    for g in range(6):
        if g == ANSWER_AT:
            answer(gz >= LATE_BELOW)
        elif g == ANSWER_LATE:
            answer(gz < LATE_BELOW)
        for piece in range(4):
            if g < 5:
                multiply(g, piece)
            if g < 4:
                build(g + 1, (2 * piece, 2 * piece + 1))
            if g > 0:
                gather(g - 1, (piece,))

    for v in range(9):
        for n in range(4):
            low = shifted[v, n + 1, pl.ds(8, 8, stride=8), :]
            high = shifted[v, n + 1, pl.ds(8 + 71, 8, stride=8), :]
            edge_p[v, n, 0] = jnp.where(low4, turn(low, 1, 0), turn(high, 1, 0))
            edge_p[v, n, 1] = jnp.where(low4, low, high)
            edge_p[v, n, 2] = jnp.where(low4, turn(low, -1, 0), turn(high, -1, 0))

    for i in range(13):
        for w in range(2):
            for n in range(4):
                low = edge[i, w, n, pl.ds(0, 4, stride=8), :]
                high = edge[i, w, n, pl.ds(39, 4, stride=8), :]
                edge_sum[i, w, n] = jnp.concatenate([low, high], axis=0)

    for n in range(4):
        lanes = slice(128 * n, 128 * n + 128)
        top = shifted[4, n + 1, 8:136, :] + num[:, lanes]
        ordered[n] = top * (1.0 / SCALE) / (1.0 + wsum[:, lanes])
        pieces = [ordered[n, pl.ds(c, 16, stride=8), :] for c in range(8)]
        out_ref[4 * n:4 * n + 4] = jnp.concatenate(pieces, axis=0).T.reshape(4, 32, 128)
    column = iota((4, 32, 128), 2)
    is_rim = (column < 4) | (column >= 124)

    got_across = jnp.logical_and(even, gz < direct_to)

    @pl.when(got_across)
    def _():
        for copy, dst, dz, dx, dy in across_copies:
            pl.when(there(-dz, -dx, -dy))(copy.wait_recv)
        for k in range(6):
            rows_h[4, k] = jnp.concatenate([yp_lo[k], yp_hi[k]], axis=0)
        from_rim = []
        for j in range(3):
            lower = jnp.concatenate([yx_lo[j], yx_hi[j]], axis=0)
            upper = jnp.concatenate([yx_lo[3 + j], yx_hi[3 + j]], axis=0)
            from_rim.append(jnp.where(lane8 % 8 < 4, lower, upper))
        rows_h[4, 6] = turn(jnp.where(lane8 >= 96, from_rim[0], from_rim[1]), 32, 1)
        rows_h[4, 7] = turn(jnp.where(lane8 >= 32, from_rim[1], from_rim[2]), -32, 1)

    @pl.when(jnp.logical_not(got_across))
    def _():
        for copy, dst, dz, dx, dy in row_copies:
            pl.when(there(0, 0, -dy))(copy.wait_recv)
        for k in range(8):
            rows_h[4, k] = jnp.concatenate([yr_lo[k], yr_hi[k]], axis=0)

    for dx in (-1, 1):
        v = 4 + dx
        for k in range(6):
            value = turn(rows_h[4, k], -dx, 1)
            edge_lane = 31 if dx == 1 else 0
            source = rows_h[4, 6 + k // 4]
            first_z = 4 * k - 8 * (k // 4)
            for j in range(4):
                src_lane = (first_z + j) * 8 + (0 if dx == 1 else 7)
                dst_lane = 32 * j + edge_lane
                value = jnp.where(lane8 == dst_lane, turn(source, dst_lane - src_lane, 1), value)
            rows_h[v, k] = value
        for m in range(2):
            value = turn(rows_h[4, 6 + m], -dx, 1)
            if m == 1:
                value = jnp.where(lane8 < 64, turn(rows_h[v, 6], 64, 1), value)
            for zz in range(8 * m, 16):
                k = 2 * m + zz // 4
                src_lane = 32 * (zz % 4) + (0 if dx == 1 else 31)
                dst_lane = 8 * zz + (7 if dx == 1 else 0)
                value = jnp.where(lane8 == dst_lane, turn(rows_h[4, k], dst_lane - src_lane, 1), value)
            rows_h[v, 6 + m] = value
    for dx in (-1, 0, 1):
        for k in range(6):
            here = turn(rows_h[4 + dx, k], -32, 1)
            after = turn(rows_h[4 + dx, k + 1], -32, 1) if k < 5 else here
            rows_h[7 + dx, k] = jnp.where(lane8 < 96, here, after)
            if 1 <= k <= 4:
                here = turn(rows_h[4 + dx, k], 32, 1)
                before = turn(rows_h[4 + dx, k - 1], 32, 1)
                rows_h[1 + dx, k] = jnp.where(lane8 >= 32, here, before)
        for m in range(2):
            rows_h[7 + dx, 6 + m] = turn(rows_h[4 + dx, 6 + m], -8, 1)
    for v in range(4, 9):
        mark = jnp.where(lane8 == 120 + v - 4, 1.0, 0.0) if v > 4 else 0.0
        for m in range(2):
            rows_h[v, 6 + m] = jnp.where(lane8 >= 120, mark, rows_h[v, 6 + m])

    for k in range(8):
        lanes = at_lanes(k)

        def inner_low(v):
            first = turn(shifted[v, k, 8:16, :], 3, 0)
            return jnp.where(low4, jnp.where(sub == 3, first, turn(rows_h[v, k], -1, 0)), rows_h[v, k])

        def inner_high(v):
            last = turn(shifted[v, k, 128:136, :], -3, 0)
            return jnp.where(low4, rows_h[v, k], jnp.where(sub == 4, last, turn(rows_h[v, k], 1, 0)))

        base, base_low, base_high = rows_h[4, k], inner_low(4), inner_high(4)
        for g in range(5):
            v = g + 4
            if g:
                moved, moved_low, moved_high = rows_h[v, k], inner_low(v), inner_high(v)
            else:
                moved, moved_low, moved_high = base, base_low, base_high
            for d, dy in enumerate(steps(g)):
                if dy == 0:
                    diff = base - moved
                elif dy == 1:
                    diff = base_high - moved_low
                else:
                    diff = base_low - moved_high
                square = diff * diff
                high = square.astype(BF16).astype(F32)
                i = offset_index(g, d)
                lhs_h[16 * i:16 * i + 16, lanes] = jnp.concatenate([high, square - high], axis=0).astype(BF16)

    for g in range(5):
        first, rows = (0, 208) if g == 0 else (16 * offset_index(g, 0), 48)
        for half in range(2):
            total = jnp.dot(lhs_h[first:first + rows, 384 * half:384 * half + 640], box[g, half], preferred_element_type=F32)
            for part in range(2):
                dist_h[1 if g else 0, 2 * half + part, first:first + rows, :] = total[:, 128 * part:128 * part + 128]

    keep_lo = jnp.where((sub == 0) & (gy == 0), 0.0, 1.0)
    keep_hi = jnp.where((sub == 7) & (gy == ny - 1), 0.0, 1.0)

    def edge_weights(i, w, dy, n, w_at):
        x = dist_h[w, n, 16 * i:16 * i + 8, :] + dist_h[w, n, 16 * i + 8:16 * i + 16, :]
        inward = jnp.where((sub == 3) | (sub == 4), 0.0, jnp.where(low4, turn(x, -1, 0), turn(x, 1, 0)))
        x = x + inward
        inward = jnp.where((sub >= 2) & (sub < 6), 0.0, jnp.where(low4, turn(x, -2, 0), turn(x, 2, 0)))
        x = x + inward
        fewer = jnp.where((sub == 3) | (sub == 4), 0.0, jnp.where(low4, turn(x, -1, 0), turn(x, 1, 0)))
        if dy == 0:
            halo = fewer
        elif (dy == 1) == (w_at == 0):
            halo = jnp.where(low4, fewer, x)
        else:
            halo = jnp.where(low4, x, fewer)
        return jnp.exp2(edge_sum[i, w_at, n] + halo)

    for n in range(4):
        def partner(v, dy):
            value = edge_p[v, n, 1 + dy]
            if dy == 1:
                return jnp.where(sub == 7, turn(rows_h[v, n + 1], 3, 0), value)
            if dy == -1:
                return jnp.where(sub == 0, turn(rows_h[v, n + 1], -3, 0), value)
            return value

        total, total_w = edge_p[4, n, 1], jnp.ones((8, 128), F32)
        for g in range(5):
            for d, dy in enumerate(steps(g)):
                i = offset_index(g, d)
                ahead = edge_weights(i, 0, dy, n, 0)
                behind = edge_weights(i, 1 if g else 0, dy, n, 1)
                if dy == 1:
                    ahead, behind = ahead * keep_hi, behind * keep_lo
                elif dy == -1:
                    ahead, behind = ahead * keep_lo, behind * keep_hi
                total = total + (ahead * partner(g + 4, dy) + behind * partner(4 - g, -dy))
                total_w = total_w + (ahead + behind)
        rim_rows = total * (1.0 / SCALE) / total_w

        columns = jnp.concatenate([rim_rows, jnp.zeros((112, 128), F32), rim_rows], axis=0).T.reshape(4, 32, 128)
        out_ref[4 * n:4 * n + 4] = jnp.where(is_rim, columns, out_ref[4 * n:4 * n + 4])

    for copy, dst, dz, dx, dy in plane_copies:
        pl.when(there(dz, dx, dy))(copy.wait_send)
    for copy, dst, dz, dx, dy in across_copies:
        pl.when(across_sent(dz, dx, dy))(copy.wait_send)
    for copy, dst, dz, dx, dy in row_copies:
        pl.when(jnp.logical_and(there(dz, dx, dy), jnp.logical_or(even, gz >= direct_to)))(copy.wait_send)


def shards(tables, noisy):
    def vmem(*shape, dtype=F32):
        return pltpu.VMEM(shape, dtype)

    return pl.pallas_call(
        kernel,
        out_shape=jax.ShapeDtypeStruct(noisy.shape, F32),
        in_specs=[pl.BlockSpec(memory_space=pl.ANY)] * 2,
        out_specs=pl.BlockSpec(memory_space=pltpu.VMEM),
        scratch_shapes=[
            vmem(26, PITCH, 128),
            vmem(16, 4, 128), vmem(16, 4, 128), vmem(24, 4, 128), vmem(24, 4, 128),
            vmem(5, 4, 128), vmem(5, 4, 128),
            vmem(6, 4, 128), vmem(6, 4, 128), vmem(6, 4, 128), vmem(6, 4, 128),
            vmem(8, 4, 128), vmem(8, 4, 128), vmem(8, 4, 128), vmem(8, 4, 128),
            vmem(9, 8, 144, 128),
            vmem(9, 8, 8, 128),
            vmem(5, 2, 640, 256, dtype=BF16),
            vmem(2, 384, 1024, dtype=BF16), vmem(2, 2, 4, 384, 128),
            vmem(128, 512), vmem(128, 512),
            vmem(208, 1024, dtype=BF16), vmem(2, 4, 208, 128),
            vmem(13, 2, 4, 64, 128), vmem(13, 2, 4, 8, 128), vmem(9, 4, 3, 8, 128),
            vmem(4, 128, 128),
            pltpu.SemaphoreType.DMA((2,)),
            pltpu.SemaphoreType.DMA((28,)),
            pltpu.SemaphoreType.DMA((28,)),
            pltpu.SemaphoreType.REGULAR,
        ],
        compiler_params=pltpu.CompilerParams(collective_id=0, has_side_effects=True, vmem_limit_bytes=54848 << 10),
    )(noisy, jnp.asarray(tables))


def solution(mesh):
    placed = P("gz", "gx", "gy")
    return jax.shard_map(
        functools.partial(shards, box_tables()), mesh=mesh, in_specs=(placed,), out_specs=placed, check_vma=False
    )
```

```python
import functools
import math

import jax
import jax.numpy as jnp
import ml_dtypes
import numpy as np
from jax import lax
from jax.experimental import pallas as pl
from jax.experimental.pallas import tpu as pltpu
from jax.sharding import PartitionSpec as P

GROUPS = ((0, 0), (0, 1), (1, -1), (1, 0), (1, 1))
VARIANTS = tuple((dz, dx) for dz in (-1, 0, 1) for dx in (-1, 0, 1))
SCALE = math.sqrt(math.log2(math.e) / 343.0)
SZ, SX, SY = 16, 32, 128
BASE, PITCH = 16, 64
MASKED = -1000.0
ANSWER_AT, ANSWER_LATE, LATE_BELOW = 2, 4, 2
ROWS_FIRST_BELOW = 3
MESH = pl.DeviceIdType.MESH
F32, BF16 = jnp.float32, jnp.bfloat16


def box_tables():
    n = np.arange(256)
    lane = np.arange(1024)
    rim = (lane < 128) | (lane >= 896)
    k, s = lane - 128, lane % 8
    zl = np.where(rim, lane % 128 // 8 + np.where(lane < 128, 0, 8), k // 32)
    xl = np.where(rim, np.where(s < 4, 32 + s, s - 8), k % 32)
    real = ~(rim & (lane % 128 >= 120))
    tables = []
    for dz, dx in GROUPS:
        halves = []
        for half in range(2):
            near = (abs(zl[:, None] - (4 + 8 * half + n // 32 - dz)) <= 3) & (abs(xl[:, None] - (n % 32 - dx)) <= 3)
            near = near & real[:, None]
            halves.append(-near[384 * half:384 * half + 640].astype(np.float32))
        tables.append(np.stack(halves))
    return np.stack(tables).astype(ml_dtypes.bfloat16)


def iota(shape, dim):
    return lax.broadcasted_iota(jnp.int32, shape, dim)


def kernel(x_ref, box_hbm, out_ref, ext, xs_lo, xs_hi, xp, xm, ys_lo, ys_hi, yp_lo, yp_hi, yx_lo, yx_hi, ye_lo, ye_hi, yr_lo, yr_hi,
           shifted, rows_h, box, lhs, dist, num, wsum, lhs_h, dist_h, edge, edge_sum, edge_p, ordered, local_sem, send_sem, recv_sem, ready):
    gx, gy, gz = lax.axis_index("gx"), lax.axis_index("gy"), lax.axis_index("gz")
    nx, ny, nz = lax.axis_size("gx"), lax.axis_size("gy"), lax.axis_size("gz")
    even = gy % 2 == 0
    odd_side = gy % 2 == 1

    def there(dz, dx, dy):
        ok = None
        for at, size, step in ((gz, nz, dz), (gx, nx, dx), (gy, ny, dy)):
            if step:
                inside = at > 0 if step < 0 else at < size - 1
                ok = inside if ok is None else jnp.logical_and(ok, inside)
        return ok

    def device(dz, dx, dy):
        return (gx + dx, gy + dy, gz + dz)

    around = [(dz, dx) for dz in (-1, 0, 1) for dx in (-1, 0, 1)]
    beside = [o for o in around if o != (0, 0)]
    barrier = pltpu.get_barrier_semaphore()
    direct_to = nz - 3
    for dy in (-1, 1):
        for dz, dx in around:
            greets = jnp.logical_and(even, there(dz, dx, dy))
            if (dz, dx) != (0, 0):
                greets = jnp.logical_and(greets, gz < direct_to)

            @pl.when(greets)
            def _():
                pl.semaphore_signal(barrier, inc=1, device_id=device(dz, dx, dy), device_id_type=MESH)
    for dz, dx in beside:
        @pl.when(there(dz, dx, 0))
        def _():
            pl.semaphore_signal(barrier, inc=1, device_id=device(dz, dx, 0), device_id_type=MESH)

    def count(at, size):
        return (at > 0).astype(jnp.int32) + (at < size - 1).astype(jnp.int32)

    n_plane = (1 + count(gz, nz)) * (1 + count(gx, nx))
    n_beside = count(gy, ny)
    n_direct = sum(((gz + dz >= 0) & (gz + dz < direct_to)).astype(jnp.int32) for dz in (-1, 0, 1))
    n_across = n_beside * (n_direct * (1 + count(gx, nx)) + (gz >= direct_to).astype(jnp.int32))

    own = pltpu.make_async_copy(x_ref, ext.at[pl.ds(4, SZ), pl.ds(BASE, SX), :], local_sem.at[0])
    own.start()
    tables = [pltpu.make_async_copy(box_hbm, box, local_sem.at[1])]

    send_z = {-1: pl.ds(0, 4), 0: pl.ds(0, 16), 1: pl.ds(12, 4)}
    land_z = {-1: pl.ds(20, 4), 0: pl.ds(4, 16), 1: pl.ds(0, 4)}

    def plane_parts(dz, dx):
        if dx == 0:
            return ext.at[pl.ds(4 + send_z[dz].start, 4), pl.ds(BASE, SX), :], ext.at[land_z[dz], pl.ds(BASE, SX), :]
        if dx == -1:
            return xs_lo.at[send_z[dz]], xp.at[land_z[dz]]
        return xs_hi.at[send_z[dz]], xm.at[land_z[dz]]

    def across_parts(dz, dx, dy):
        src, dst_p, dst_x = (ys_lo, yp_hi, yx_hi) if dy == -1 else (ys_hi, yp_lo, yx_lo)
        if dx == 0:
            tiles = {-1: pl.ds(0, 1), 0: pl.ds(0, 4), 1: pl.ds(3, 1)}[dz]
            land = {-1: pl.ds(5, 1), 0: pl.ds(1, 4), 1: pl.ds(0, 1)}[dz]
            return src.at[tiles], dst_p.at[land]
        return src.at[pl.ds(4, 1)], dst_x.at[pl.ds((0 if dx == -1 else 3) + 1 - dz, 1)]

    plane_copies, across_copies = [], []
    for dz, dx in beside:
        src, dst = plane_parts(dz, dx)
        i = len(plane_copies)
        copy = pltpu.make_async_remote_copy(
            src_ref=src, dst_ref=dst, send_sem=send_sem.at[i], recv_sem=recv_sem.at[i],
            device_id=device(dz, dx, 0), device_id_type=MESH)
        plane_copies.append((copy, dst, dz, dx, 0))
    for dy in (-1, 1):
        for dz, dx in sorted(around, key=lambda o: -abs(o[0]) - abs(o[1])):
            src, dst = across_parts(dz, dx, dy)
            i = 10 + len(across_copies)
            copy = pltpu.make_async_remote_copy(
                src_ref=src, dst_ref=dst, send_sem=send_sem.at[i], recv_sem=recv_sem.at[i],
                device_id=device(dz, dx, dy), device_id_type=MESH)
            across_copies.append((copy, dst, dz, dx, dy))
    row_copies = []
    for i, (dy, src, dst) in enumerate(((-1, ye_lo, yr_hi), (1, ye_hi, yr_lo))):
        copy = pltpu.make_async_remote_copy(
            src_ref=src, dst_ref=dst, send_sem=send_sem.at[8 + i], recv_sem=recv_sem.at[8 + i],
            device_id=device(0, 0, dy), device_id_type=MESH)
        row_copies.append((copy, dst, 0, 0, dy))

    lane = iota((128, 128), 1)
    low_half = iota((8, 128), 0) < 4

    def block(v, k):
        dz, dx = VARIANTS[v]
        if k < 6:
            return jnp.concatenate([ext[4 * k + j + dz, BASE + dx:BASE + 32 + dx, :] for j in range(4)], axis=0)
        pieces = []
        for j in range(16):
            zi = 8 * (k - 6) + j + dz
            pieces.append(jnp.where(low_half, ext[zi, BASE + 32 + dx:BASE + 40 + dx, :], ext[zi, BASE - 8 + dx:BASE + dx, :]))
        return jnp.concatenate(pieces, axis=0)

    def place(v, k):
        whole = turned = (block(v, k) * SCALE).T
        if k >= 6:
            mark = jnp.where(lane == 120 + v - 4, 1.0, 0.0) if v > 4 else 0.0
            turned = jnp.where(lane >= 120, mark, turned)
        for c in range(8):
            shifted[v, k, pl.ds(8 + c, 16, stride=8), :] = turned[16 * c:16 * c + 16]
        return whole

    pl.semaphore_wait(barrier, n_plane - 1 + n_across * odd_side.astype(jnp.int32))

    @pl.when(odd_side)
    def _():
        for dy in (-1, 1):
            @pl.when(there(0, 0, dy))
            def _():
                pl.semaphore_signal(ready, inc=1, device_id=device(0, 0, dy), device_id_type=MESH)

    own.wait()
    xs_lo[...] = ext[4:20, BASE:BASE + 4, :]
    xs_hi[...] = ext[4:20, BASE + 28:BASE + 32, :]
    rows_first = jnp.logical_and(odd_side, gz < ROWS_FIRST_BELOW)

    def send_planes():
        for copy, dst, dz, dx, dy in plane_copies:
            pl.when(there(dz, dx, 0))(copy.start)

    pl.when(jnp.logical_not(rows_first))(send_planes)
    for copy in tables:
        copy.start()
    def place_and_keep(v, k):
        turned = place(v, k)
        if v == 4:
            ye_lo[k] = turned[0:4]
            ye_hi[k] = turned[124:128]
            if 1 <= k <= 4:
                ys_lo[k - 1] = turned[0:4]
                ys_hi[k - 1] = turned[124:128]

    for k in range(1, 5):
        place_and_keep(4, k)
    rim = jnp.concatenate([jnp.where(low_half, ext[4 + j, BASE:BASE + 8, :], ext[4 + j, BASE + 24:BASE + 32, :]) for j in range(SZ)], axis=0)
    turned = (rim * SCALE).T
    ys_lo[4] = turned[0:4]
    ys_hi[4] = turned[124:128]

    def across_sent(dz, dx, dy):
        return jnp.logical_and(jnp.logical_and(odd_side, gz + dz < direct_to), there(dz, dx, dy))

    for copy, dst, dz, dx, dy in across_copies:
        pl.when(across_sent(dz, dx, dy))(copy.start)

    pl.when(rows_first)(send_planes)
    ext[0:24, 0:BASE] = jnp.zeros((24, BASE, 128), F32)
    ext[0:24, BASE + SX:PITCH] = jnp.zeros((24, PITCH - BASE - SX, 128), F32)
    ext[24:26] = jnp.zeros((2, PITCH, 128), F32)
    for copy, dst, dz, dx, dy in plane_copies + row_copies + across_copies:
        @pl.when(jnp.logical_not(there(-dz, -dx, -dy)))
        def _():
            dst[...] = jnp.zeros(dst.shape, F32)

    early = [(v, k) for v, ks in ((7, range(1, 4)), (1, range(2, 5))) for k in ks]
    for v, k in early:
        place(v, k)

    for copy in tables:
        copy.wait()
    row = iota((16, 256), 0) - 8
    col = iota((16, 256), 1)
    row_dz = jnp.where(row >= 2, 1, 0)
    row_dx = jnp.where(row == 1, 1, jnp.where((row >= 2) & (row < 5), row - 3, 0))
    known = (row >= 1) & (row < 5)
    for half in range(2):
        vz = gz * SZ + 8 * half + col // 32
        vx = gx * SX + col % 32

        def outside(sign):
            z, x = vz + sign * row_dz, vx + sign * row_dx
            return (z < 0) | (z >= nz * SZ) | (x < 0) | (x >= nx * SX)

        mask_rows = slice(112 + 512 * half, 128 + 512 * half)
        box[0, half, mask_rows, :] = jnp.where(known & outside(1), MASKED, box[0, half, mask_rows, :].astype(F32)).astype(BF16)
        back = known & outside(-1)
        for g in range(1, 5):
            box[g, half, mask_rows, :] = jnp.where(back & (row == g), MASKED, box[g, half, mask_rows, :].astype(F32)).astype(BF16)

    for copy, dst, dz, dx, dy in plane_copies:
        pl.when(there(-dz, -dx, 0))(copy.wait_recv)
    ext[0:24, BASE + 32:BASE + 36, :] = xp[...]
    ext[0:24, BASE - 4:BASE, :] = xm[...]
    for k in range(8):
        if k < 1 or k > 4:
            place_and_keep(4, k)

    def send_rows():
        for copy, dst, dz, dx, dy in row_copies:
            pl.when(there(0, 0, dy))(copy.start)

    pl.when(jnp.logical_and(odd_side, gz >= direct_to))(send_rows)
    for v in (5, 6, 7, 8, 0, 1, 2, 3):
        for k in (range(8) if v > 4 else range(1, 5)):
            if (v, k) not in early:
                place(v, k)

    def answer(here):
        @pl.when(jnp.logical_and(even, here))
        def _():
            pl.semaphore_wait(ready, n_beside)
            send_rows()

    lane8 = iota((8, 128), 1)
    sub = iota((8, 128), 0)

    def turn(value, by, axis):
        by = by % value.shape[axis]
        return value if by == 0 else pltpu.roll(value, by, axis)

    for v in range(9):
        for k in (range(8) if v >= 4 else range(1, 5)):
            shifted[v, k, 0:8, :] = turn(shifted[v, k, 128:136, :], 1, 0)
            shifted[v, k, 136:144, :] = turn(shifted[v, k, 8:16, :], -1, 0)

    def steps(g):
        return (1,) if g == 0 else (-1, 0, 1)

    def offset_index(g, d):
        return 0 if g == 0 else 3 * g - 2 + d

    def at_lanes(k):
        tile = k + 1 if k < 6 else 7 * (k - 6)
        return slice(128 * tile, 128 * tile + 128)

    def build(g, ks):
        v = g + 4
        for d, dy in enumerate(steps(g)):
            for k in ks:
                lanes = at_lanes(k)
                error = None
                for j in range(8):
                    diff = shifted[4, k, 8 + 16 * j:24 + 16 * j, :] - shifted[v, k, 8 + 16 * j + 8 * dy:24 + 16 * j + 8 * dy, :]
                    square = diff * diff
                    if error is not None:
                        square = square + error
                    rounded = square.astype(BF16)
                    lhs[g % 2, 128 * d + 16 * j:128 * d + 16 * j + 16, lanes] = rounded
                    error = square - rounded.astype(F32)

    def multiply(g, piece):
        rows = 128 * len(steps(g))
        half, w = piece // 2, piece % 2
        if w == 0 or g:
            table = g if w else 0
            total = jnp.dot(lhs[g % 2, 0:rows, 384 * half:384 * half + 640], box[table, half], preferred_element_type=F32)
            for part in range(2):
                dist[g % 2, w, 2 * half + part, 0:rows, :] = total[:, 128 * part:128 * part + 128]

    low4 = sub < 4

    def weights(g, w, d, dy, n, first):
        cache = {}

        def get(t):
            if t not in cache:
                if 0 <= t < 16:
                    value = dist[g % 2, w, n, 128 * d + 8 * t:128 * d + 8 * t + 8, :]
                    if t == 15 and dy == 1:
                        value = jnp.where(sub == 7, 0.0, value)
                    elif t == 0 and dy == -1:
                        value = jnp.where(sub == 0, 0.0, value)
                    cache[t] = value
                elif t < 0:
                    cache[t] = jnp.where(sub == 0, 0.0, turn(get(16 + t), 1, 0))
                else:
                    cache[t] = jnp.where(sub == 7, 0.0, turn(get(t - 16), -1, 0))
            return cache[t]

        total = get(first - 3)
        for t in range(first - 2, first + 4):
            total = total + get(t)
        result = []
        for i in range(16):
            if i:
                total = total + (get(first + i + 3) - get(first + i - 4))
            if i < 4 or i >= 12:
                at = 8 * (i if i < 4 else i - 8)
                edge[offset_index(g, d), w if g else (1 if first else 0), n, at:at + 8, :] = total
            result.append(jnp.exp2(total))
        return result

    def gather(g, ns):
        v = g + 4
        for n in ns:
            lanes = slice(128 * n, 128 * n + 128)
            for d, dy in enumerate(steps(g)):
                ahead = weights(g, 0, d, dy, n, 0)
                behind = weights(g, 1 if g else 0, d, dy, n, -dy)
                for t in range(16):
                    rows = slice(8 * t, 8 * t + 8)
                    up = shifted[v, n + 1, 8 + 8 * (t + dy):16 + 8 * (t + dy), :]
                    down = shifted[8 - v, n + 1, 8 + 8 * (t - dy):16 + 8 * (t - dy), :]
                    part = ahead[t] * up + behind[t] * down
                    part_w = ahead[t] + behind[t]
                    if g == 0:
                        num[rows, lanes] = part
                        wsum[rows, lanes] = part_w
                    else:
                        num[rows, lanes] += part
                        wsum[rows, lanes] += part_w

    build(0, range(8))
    for g in range(6):
        if g == ANSWER_AT:
            answer(gz >= LATE_BELOW)
        elif g == ANSWER_LATE:
            answer(gz < LATE_BELOW)
        for piece in range(4):
            if g < 5:
                multiply(g, piece)
            if g < 4:
                build(g + 1, (2 * piece, 2 * piece + 1))
            if g > 0:
                gather(g - 1, (piece,))

    for v in range(9):
        for n in range(4):
            low = shifted[v, n + 1, pl.ds(8, 8, stride=8), :]
            high = shifted[v, n + 1, pl.ds(8 + 71, 8, stride=8), :]
            edge_p[v, n, 0] = jnp.where(low4, turn(low, 1, 0), turn(high, 1, 0))
            edge_p[v, n, 1] = jnp.where(low4, low, high)
            edge_p[v, n, 2] = jnp.where(low4, turn(low, -1, 0), turn(high, -1, 0))

    for i in range(13):
        for w in range(2):
            for n in range(4):
                low = edge[i, w, n, pl.ds(0, 4, stride=8), :]
                high = edge[i, w, n, pl.ds(39, 4, stride=8), :]
                edge_sum[i, w, n] = jnp.concatenate([low, high], axis=0)

    for n in range(4):
        lanes = slice(128 * n, 128 * n + 128)
        top = shifted[4, n + 1, 8:136, :] + num[:, lanes]
        ordered[n] = top * (1.0 / SCALE) / (1.0 + wsum[:, lanes])
        pieces = [ordered[n, pl.ds(c, 16, stride=8), :] for c in range(8)]
        out_ref[4 * n:4 * n + 4] = jnp.concatenate(pieces, axis=0).T.reshape(4, 32, 128)
    column = iota((4, 32, 128), 2)
    is_rim = (column < 4) | (column >= 124)

    got_across = jnp.logical_and(even, gz < direct_to)

    @pl.when(got_across)
    def _():
        for copy, dst, dz, dx, dy in across_copies:
            pl.when(there(-dz, -dx, -dy))(copy.wait_recv)
        for k in range(6):
            rows_h[4, k] = jnp.concatenate([yp_lo[k], yp_hi[k]], axis=0)
        from_rim = []
        for j in range(3):
            lower = jnp.concatenate([yx_lo[j], yx_hi[j]], axis=0)
            upper = jnp.concatenate([yx_lo[3 + j], yx_hi[3 + j]], axis=0)
            from_rim.append(jnp.where(lane8 % 8 < 4, lower, upper))
        rows_h[4, 6] = turn(jnp.where(lane8 >= 96, from_rim[0], from_rim[1]), 32, 1)
        rows_h[4, 7] = turn(jnp.where(lane8 >= 32, from_rim[1], from_rim[2]), -32, 1)

    @pl.when(jnp.logical_not(got_across))
    def _():
        for copy, dst, dz, dx, dy in row_copies:
            pl.when(there(0, 0, -dy))(copy.wait_recv)
        for k in range(8):
            rows_h[4, k] = jnp.concatenate([yr_lo[k], yr_hi[k]], axis=0)

    for dx in (-1, 1):
        v = 4 + dx
        for k in range(6):
            value = turn(rows_h[4, k], -dx, 1)
            edge_lane = 31 if dx == 1 else 0
            source = rows_h[4, 6 + k // 4]
            first_z = 4 * k - 8 * (k // 4)
            for j in range(4):
                src_lane = (first_z + j) * 8 + (0 if dx == 1 else 7)
                dst_lane = 32 * j + edge_lane
                value = jnp.where(lane8 == dst_lane, turn(source, dst_lane - src_lane, 1), value)
            rows_h[v, k] = value
        for m in range(2):
            value = turn(rows_h[4, 6 + m], -dx, 1)
            if m == 1:
                value = jnp.where(lane8 < 64, turn(rows_h[v, 6], 64, 1), value)
            for zz in range(8 * m, 16):
                k = 2 * m + zz // 4
                src_lane = 32 * (zz % 4) + (0 if dx == 1 else 31)
                dst_lane = 8 * zz + (7 if dx == 1 else 0)
                value = jnp.where(lane8 == dst_lane, turn(rows_h[4, k], dst_lane - src_lane, 1), value)
            rows_h[v, 6 + m] = value
    for dx in (-1, 0, 1):
        for k in range(6):
            here = turn(rows_h[4 + dx, k], -32, 1)
            after = turn(rows_h[4 + dx, k + 1], -32, 1) if k < 5 else here
            rows_h[7 + dx, k] = jnp.where(lane8 < 96, here, after)
            if 1 <= k <= 4:
                here = turn(rows_h[4 + dx, k], 32, 1)
                before = turn(rows_h[4 + dx, k - 1], 32, 1)
                rows_h[1 + dx, k] = jnp.where(lane8 >= 32, here, before)
        for m in range(2):
            rows_h[7 + dx, 6 + m] = turn(rows_h[4 + dx, 6 + m], -8, 1)
    for v in range(4, 9):
        mark = jnp.where(lane8 == 120 + v - 4, 1.0, 0.0) if v > 4 else 0.0
        for m in range(2):
            rows_h[v, 6 + m] = jnp.where(lane8 >= 120, mark, rows_h[v, 6 + m])

    for k in range(8):
        lanes = at_lanes(k)

        def inner_low(v):
            first = turn(shifted[v, k, 8:16, :], 3, 0)
            return jnp.where(low4, jnp.where(sub == 3, first, turn(rows_h[v, k], -1, 0)), rows_h[v, k])

        def inner_high(v):
            last = turn(shifted[v, k, 128:136, :], -3, 0)
            return jnp.where(low4, rows_h[v, k], jnp.where(sub == 4, last, turn(rows_h[v, k], 1, 0)))

        base, base_low, base_high = rows_h[4, k], inner_low(4), inner_high(4)
        for g in range(5):
            v = g + 4
            if g:
                moved, moved_low, moved_high = rows_h[v, k], inner_low(v), inner_high(v)
            else:
                moved, moved_low, moved_high = base, base_low, base_high
            for d, dy in enumerate(steps(g)):
                if dy == 0:
                    diff = base - moved
                elif dy == 1:
                    diff = base_high - moved_low
                else:
                    diff = base_low - moved_high
                square = diff * diff
                high = square.astype(BF16).astype(F32)
                i = offset_index(g, d)
                lhs_h[16 * i:16 * i + 16, lanes] = jnp.concatenate([high, square - high], axis=0).astype(BF16)

    for g in range(5):
        first, rows = (0, 208) if g == 0 else (16 * offset_index(g, 0), 48)
        for half in range(2):
            total = jnp.dot(lhs_h[first:first + rows, 384 * half:384 * half + 640], box[g, half], preferred_element_type=F32)
            for part in range(2):
                dist_h[1 if g else 0, 2 * half + part, first:first + rows, :] = total[:, 128 * part:128 * part + 128]

    keep_lo = jnp.where((sub == 0) & (gy == 0), 0.0, 1.0)
    keep_hi = jnp.where((sub == 7) & (gy == ny - 1), 0.0, 1.0)

    def edge_weights(i, w, dy, n, w_at):
        x = dist_h[w, n, 16 * i:16 * i + 8, :] + dist_h[w, n, 16 * i + 8:16 * i + 16, :]
        inward = jnp.where((sub == 3) | (sub == 4), 0.0, jnp.where(low4, turn(x, -1, 0), turn(x, 1, 0)))
        x = x + inward
        inward = jnp.where((sub >= 2) & (sub < 6), 0.0, jnp.where(low4, turn(x, -2, 0), turn(x, 2, 0)))
        x = x + inward
        fewer = jnp.where((sub == 3) | (sub == 4), 0.0, jnp.where(low4, turn(x, -1, 0), turn(x, 1, 0)))
        if dy == 0:
            halo = fewer
        elif (dy == 1) == (w_at == 0):
            halo = jnp.where(low4, fewer, x)
        else:
            halo = jnp.where(low4, x, fewer)
        return jnp.exp2(edge_sum[i, w_at, n] + halo)

    for n in range(4):
        def partner(v, dy):
            value = edge_p[v, n, 1 + dy]
            if dy == 1:
                return jnp.where(sub == 7, turn(rows_h[v, n + 1], 3, 0), value)
            if dy == -1:
                return jnp.where(sub == 0, turn(rows_h[v, n + 1], -3, 0), value)
            return value

        total, total_w = edge_p[4, n, 1], jnp.ones((8, 128), F32)
        for g in range(5):
            for d, dy in enumerate(steps(g)):
                i = offset_index(g, d)
                ahead = edge_weights(i, 0, dy, n, 0)
                behind = edge_weights(i, 1 if g else 0, dy, n, 1)
                if dy == 1:
                    ahead, behind = ahead * keep_hi, behind * keep_lo
                elif dy == -1:
                    ahead, behind = ahead * keep_lo, behind * keep_hi
                total = total + (ahead * partner(g + 4, dy) + behind * partner(4 - g, -dy))
                total_w = total_w + (ahead + behind)
        rim_rows = total * (1.0 / SCALE) / total_w

        columns = jnp.concatenate([rim_rows, jnp.zeros((112, 128), F32), rim_rows], axis=0).T.reshape(4, 32, 128)
        out_ref[4 * n:4 * n + 4] = jnp.where(is_rim, columns, out_ref[4 * n:4 * n + 4])

    for copy, dst, dz, dx, dy in plane_copies:
        pl.when(there(dz, dx, dy))(copy.wait_send)
    for copy, dst, dz, dx, dy in across_copies:
        pl.when(across_sent(dz, dx, dy))(copy.wait_send)
    for copy, dst, dz, dx, dy in row_copies:
        pl.when(jnp.logical_and(there(dz, dx, dy), jnp.logical_or(even, gz >= direct_to)))(copy.wait_send)


def shards(tables, noisy):
    def vmem(*shape, dtype=F32):
        return pltpu.VMEM(shape, dtype)

    return pl.pallas_call(
        kernel,
        out_shape=jax.ShapeDtypeStruct(noisy.shape, F32),
        in_specs=[pl.BlockSpec(memory_space=pl.ANY)] * 2,
        out_specs=pl.BlockSpec(memory_space=pltpu.VMEM),
        scratch_shapes=[
            vmem(26, PITCH, 128),
            vmem(16, 4, 128), vmem(16, 4, 128), vmem(24, 4, 128), vmem(24, 4, 128),
            vmem(5, 4, 128), vmem(5, 4, 128),
            vmem(6, 4, 128), vmem(6, 4, 128), vmem(6, 4, 128), vmem(6, 4, 128),
            vmem(8, 4, 128), vmem(8, 4, 128), vmem(8, 4, 128), vmem(8, 4, 128),
            vmem(9, 8, 144, 128),
            vmem(9, 8, 8, 128),
            vmem(5, 2, 640, 256, dtype=BF16),
            vmem(2, 384, 1024, dtype=BF16), vmem(2, 2, 4, 384, 128),
            vmem(128, 512), vmem(128, 512),
            vmem(208, 1024, dtype=BF16), vmem(2, 4, 208, 128),
            vmem(13, 2, 4, 64, 128), vmem(13, 2, 4, 8, 128), vmem(9, 4, 3, 8, 128),
            vmem(4, 128, 128),
            pltpu.SemaphoreType.DMA((2,)),
            pltpu.SemaphoreType.DMA((28,)),
            pltpu.SemaphoreType.DMA((28,)),
            pltpu.SemaphoreType.REGULAR,
        ],
        compiler_params=pltpu.CompilerParams(collective_id=0, has_side_effects=True, vmem_limit_bytes=54848 << 10),
    )(noisy, jnp.asarray(tables))


def solution(mesh):
    placed = P("gz", "gx", "gy")
    return jax.shard_map(
        functools.partial(shards, box_tables()), mesh=mesh, in_specs=(placed,), out_specs=placed, check_vma=False
    )
```
